512 devices in a mesh: gx: 32 (over x_lo, z, core), gy: 8 (over y), gz: 2 (over x_hi).
Axes of the slice: x: 4 (x_hi: 2, x_lo: 2; x = x_hi * 2 + x_lo), y: 8, z: 8, core: 2. Of those that a mesh axis runs over, the one named last changes fastest.
Arguments:
- noisy_volume: float32 [256, 256, 256], P('gx', 'gy', 'gz'), may hold values from -8 to 8
- primal: float32 [256, 256, 256], P('gx', 'gy', 'gz'), may hold values from -6 to 6
- dual_field: float32 [3, 256, 256, 256], P(None, 'gx', 'gy', 'gz'), may hold values from -0.3 to 0.3
Outputs:
- denoised: float32 [256, 256, 256], P('gx', 'gy', 'gz')
- dual_final: float32 [3, 256, 256, 256], P(None, 'gx', 'gy', 'gz')
- residual_norms: float32 [2], replicated
The draws below stay inside these ranges and needn't reach their ends.
All inputs are finite; a program needn't handle non-finite values.
Results may differ from the reference program's by a relative error of at most 0.0001.
Values sent between devices are 32-bit elements; how exact they have to be, the bound alone decides.
No kernel may reach another device: no remote copies, remote signals or barrier semaphores. Data moves between devices by JAX's collectives and lax.ppermute only.
A program may use at most 64 MiB of HBM per device.

```python
import math
import jax
import jax.numpy as jnp
from jax import lax

ITERS = 2
NX = 256
NY = 256
NZ = 256


def draw_noisy_volume(key, part):
    key = jax.random.fold_in(key, 7)
    key_phase, key_noise = jax.random.split(key, 2)
    phases = jax.random.uniform(key_phase, (3,), jnp.float32) * (2.0 * math.pi)
    coord_x = jnp.arange(NX, dtype=jnp.float32)[:, None, None]
    coord_y = jnp.arange(NY, dtype=jnp.float32)[None, :, None]
    coord_z = jnp.arange(NZ, dtype=jnp.float32)[None, None, :]
    ramp = 1.0 + 2.0 * coord_x / float(max(NX - 1, 1))
    pattern = jnp.sin(2.0 * math.pi * 3.0 * coord_x / NX + phases[0]) * jnp.cos(2.0 * math.pi * 2.0 * coord_y / NY + phases[1]) * jnp.sin(2.0 * math.pi * 2.0 * coord_z / NZ + phases[2])
    noise = jnp.clip(jax.random.normal(key_noise, (NX, NY, NZ), jnp.float32), -4.0, 4.0)
    result = pattern + 0.4 * ramp * noise
    return result.astype(jnp.float32)


def level_of(own_key, shape, shards, least, largest):
    level, own = 1.0, jax.random.fold_in(own_key, 6)
    for position, shards_of in shards:
        heights = jnp.exp(jax.random.uniform(jax.random.fold_in(own, position), (shards_of,), jnp.float32, least / len(shards), largest / len(shards)))
        level = level * jnp.repeat(heights, shape[position] // shards_of).reshape([-1 if axis == position else 1 for axis in range(len(shape))])
    return level


def gaussian(stream_key, dims, width, bound, pieces=(), held_as=jnp.bfloat16):
    values = jax.random.normal(stream_key, dims, jnp.float32) * width
    if len(pieces) > 0:
        values = level_of(stream_key, dims, pieces, -0.22, 0.18) * values
    return jnp.clip(values, min=-bound, max=bound).astype(held_as)


def setup_inputs(seed: int = 0) -> dict:
    seeds = jax.random.split(jax.random.key(seed), 4)
    noisy_volume = draw_noisy_volume(jax.random.fold_in(seeds[3], 71), 0)
    primal = gaussian(seeds[1], (NX, NY, NZ), 1.0, 6.0, ((0, 32), (1, 8), (2, 2)), jnp.float32)
    dual_field = jnp.clip(jax.random.uniform(seeds[2], (3, NX, NY, NZ), jnp.float32, -0.3, 0.3) * level_of(seeds[2], (3, NX, NY, NZ), ((1, 32), (2, 8), (3, 2)), -0.4, 0.0), -0.3, 0.3)
    return {"noisy_volume": noisy_volume, "primal": primal, "dual_field": dual_field}


step_primal = 0.25
step_dual = 0.3
radius_tv = 0.5

def advance(source, current, leading, dual_pad, anchor, extent):
    size_x, size_y, size_z = leading.shape
    centre_vals = leading[:-1, :-1, :-1]
    gradient = jnp.stack([leading[1:, :-1, :-1] - centre_vals, leading[:-1, 1:, :-1] - centre_vals, leading[:-1, :-1, 1:] - centre_vals])
    index_x = anchor[0] + jnp.arange(size_x - 1, dtype=jnp.int32)
    index_y = anchor[1] + jnp.arange(size_y - 1, dtype=jnp.int32)
    index_z = anchor[2] + jnp.arange(size_z - 1, dtype=jnp.int32)
    inside_x = ((index_x >= 0) & (index_x <= extent[0] - 2))[:, None, None]
    inside_y = ((index_y >= 0) & (index_y <= extent[1] - 2))[None, :, None]
    inside_z = ((index_z >= 0) & (index_z <= extent[2] - 2))[None, None, :]
    shape_out = centre_vals.shape
    inside_mask = jnp.stack([jnp.broadcast_to(inside_x, shape_out), jnp.broadcast_to(inside_y, shape_out), jnp.broadcast_to(inside_z, shape_out)])
    gradient = jnp.where(inside_mask, gradient, 0.0)
    moved = dual_pad[:, :-1, :-1, :-1] + step_dual * gradient
    magnitude = jnp.sqrt(lax.optimization_barrier(jnp.sum(moved * moved, axis=0)))
    shrinkage = jnp.maximum(1.0, magnitude / radius_tv)
    projected = jnp.where(inside_mask, moved / shrinkage, 0.0)
    divergence = projected[0, 1:, 1:, 1:] - projected[0, :-1, 1:, 1:] + projected[1, 1:, 1:, 1:] - projected[1, 1:, :-1, 1:] + projected[2, 1:, 1:, 1:] - projected[2, 1:, 1:, :-1]
    updated = (current + step_primal * (divergence + source)) / (1.0 + step_primal)
    return (updated, 2.0 * updated - current, projected[:, 1:, 1:, 1:])

def reference(noisy_volume, primal, dual_field):
    current = primal
    leading = primal
    dual_now = dual_field
    history = []
    for turn in range(ITERS):
        lead_pad = jnp.pad(leading, ((1, 1), (1, 1), (1, 1)))
        dual_pad = jnp.pad(dual_now, ((0, 0), (1, 1), (1, 1), (1, 1)))
        updated, leading, dual_new = advance(noisy_volume, current, lead_pad, dual_pad, (-1, -1, -1), (NX, NY, NZ))
        change = jnp.sum((updated - current) ** 2) / step_primal + jnp.sum((dual_new - dual_now) ** 2) / step_dual
        history.append(change)
        current = updated
        dual_now = dual_new
    cells = float(NX * NY * NZ)
    return (current, dual_now, jnp.sqrt(jnp.stack(history) / cells))
```

```python
import jax
import jax.numpy as jnp
from jax import lax
from jax.sharding import Mesh, PartitionSpec as P

ITERS = 2
GX = ("xl", "z", "core")
GY = "y"
GZ = "xh"


step_primal = 0.25
step_dual = 0.3
radius_tv = 0.5


def extended(cells, sides, width):
    for axis, dim in sides:
        count = lax.axis_size(axis)
        ends = count - 1
        head = lax.slice_in_dim(cells, 0, width, axis=dim)
        tail = lax.slice_in_dim(cells, cells.shape[dim] - width, cells.shape[dim], axis=dim)
        cells = jnp.concatenate(
            [
                lax.ppermute(tail, axis, [(i, (i + 1) % count) for i in range(ends)]),
                cells,
                lax.ppermute(head, axis, [((i + 1) % count, i) for i in range(ends)]),
            ],
            axis=dim,
        )
    return cells


def advance(source, current, leading, dual_pad, anchor, extent):
    size_x, size_y, size_z = leading.shape
    centre_vals = leading[:-1, :-1, :-1]
    gradient = jnp.stack(
        [
            leading[1:, :-1, :-1] - centre_vals,
            leading[:-1, 1:, :-1] - centre_vals,
            leading[:-1, :-1, 1:] - centre_vals,
        ]
    )
    index_x = anchor[0] + jnp.arange(size_x - 1, dtype=jnp.int32)
    index_y = anchor[1] + jnp.arange(size_y - 1, dtype=jnp.int32)
    index_z = anchor[2] + jnp.arange(size_z - 1, dtype=jnp.int32)
    inside_x = ((index_x >= 0) & (index_x <= extent[0] - 2))[:, None, None]
    inside_y = ((index_y >= 0) & (index_y <= extent[1] - 2))[None, :, None]
    inside_z = ((index_z >= 0) & (index_z <= extent[2] - 2))[None, None, :]
    shape_out = centre_vals.shape
    inside_mask = jnp.stack(
        [
            jnp.broadcast_to(inside_x, shape_out),
            jnp.broadcast_to(inside_y, shape_out),
            jnp.broadcast_to(inside_z, shape_out),
        ]
    )
    gradient = jnp.where(inside_mask, gradient, 0.0)
    moved = dual_pad[:, :-1, :-1, :-1] + step_dual * gradient
    magnitude = jnp.sqrt(jnp.sum(moved * moved, axis=0))
    shrinkage = jnp.maximum(1.0, magnitude / radius_tv)
    projected = jnp.where(inside_mask, moved / shrinkage, 0.0)
    divergence = (
        projected[0, 1:, 1:, 1:]
        - projected[0, :-1, 1:, 1:]
        + projected[1, 1:, 1:, 1:]
        - projected[1, 1:, :-1, 1:]
        + projected[2, 1:, 1:, 1:]
        - projected[2, 1:, 1:, :-1]
    )
    updated = (current + step_primal * (divergence + source)) / (1.0 + step_primal)
    return (updated, 2.0 * updated - current, projected[:, 1:, 1:, 1:])


def settle(values):
    for axes in (("xl", "core", "xh"), ("z", "y")):
        count = lax.axis_size(axes)
        spread = jnp.broadcast_to(values[None], (count,) + values.shape)
        values = jnp.sum(lax.all_to_all(spread, axes, 0, 0), axis=0)
    return values


def on_device(noisy_volume, primal, dual_field):
    cells_x, cells_y, cells_z = noisy_volume.shape
    start_x = lax.axis_index(GX) * cells_x
    start_y = lax.axis_index(GY) * cells_y
    start_z = lax.axis_index(GZ) * cells_z
    extent = (
        cells_x * lax.axis_size(GX),
        cells_y * lax.axis_size(GY),
        cells_z * lax.axis_size(GZ),
    )
    history = []
    current = primal
    leading = primal
    dual_now = dual_field
    for turn in range(ITERS):
        stacked = jnp.concatenate([leading[None], dual_now], axis=0)
        padded = extended(stacked, ((GX, 1), (GY, 2), (GZ, 3)), 1)
        lead_pad = padded[0]
        dual_pad = padded[1:]
        updated, leading, dual_new = advance(
            noisy_volume,
            current,
            lead_pad,
            dual_pad,
            (start_x - 1, start_y - 1, start_z - 1),
            extent,
        )
        local_sum = (
            jnp.sum((updated - current) ** 2) / step_primal
            + jnp.sum((dual_new - dual_now) ** 2) / step_dual
        )
        history.append(local_sum)
        current = updated
        dual_now = dual_new
    sums = settle(jnp.stack(history))
    cells = float(extent[0] * extent[1] * extent[2])
    return (current, dual_now, jnp.sqrt(sums / cells))


def solution(mesh):
    mesh = Mesh(mesh.devices.reshape(2, 8, 2, 8, 2), ("xl", "z", "core", "y", "xh"))
    placed = (P(GX, GY, GZ), P(GX, GY, GZ), P(None, GX, GY, GZ))
    return jax.shard_map(
        on_device,
        mesh=mesh,
        in_specs=placed,
        out_specs=(P(GX, GY, GZ), P(None, GX, GY, GZ), P()),
        check_vma=False,
    )
```

```python
import jax
import jax.numpy as jnp
from jax import lax
from jax.experimental import pallas as pl
from jax.experimental.pallas import tpu as pltpu
from jax.sharding import Mesh, PartitionSpec as P


GX = ("xl", "z", "core")
GY = "y"
GZ = "xh"
SIZES = (2, 8, 2, 8, 2)

STEP_PRIMAL = 0.25
STEP_DUAL = 0.3
RADIUS = 0.5
OWN = 8
ROWS = 32
ALL_ROWS = 40
LANES = 128
GROUP = 24

VMEM = pl.BlockSpec(memory_space=pltpu.VMEM)


def lanes_of(rows):
    return lax.broadcasted_iota(jnp.int32, (rows, LANES), 1)


def rows_of(rows):
    return lax.broadcasted_iota(jnp.int32, (rows, LANES), 0)


def fields(u_ref, p_ref, f_ref):
    return (u_ref, p_ref.at[0], p_ref.at[1], p_ref.at[2], f_ref)


def z_faces(u_ref, f_ref, p_ref, out_ref):
    first = 1 - lax.axis_index(GZ)
    pair = lanes_of(ROWS) >> 1
    columns = jnp.zeros((ROWS, LANES), jnp.float32)
    for g, field in enumerate(fields(u_ref, p_ref, f_ref)):
        for x in range(OWN):
            lane = g * GROUP + 2 * (x + 2)
            moved = pltpu.roll(field[x], lane + 2 * first, 1)
            columns = jnp.where(pair == lane // 2, moved, columns)
    out_ref[...] = columns


def y_faces(u_ref, f_ref, p_ref, columns_ref, up_ref, down_ref):
    up_ref[0] = u_ref[:, ROWS - 2, :]
    up_ref[1] = u_ref[:, ROWS - 1, :]
    down_ref[0] = u_ref[:, 0, :]
    down_ref[1] = u_ref[:, 1, :]
    for d in range(3):
        up_ref[2 + d] = p_ref[d, :, ROWS - 2, :]
        up_ref[5 + d] = p_ref[d, :, ROWS - 1, :]
        down_ref[2 + d] = p_ref[d, :, 0, :]
    up_ref[8] = f_ref[:, ROWS - 1, :]
    down_ref[5] = f_ref[:, 0, :]
    up_ref[9] = columns_ref[ROWS - 8 :, :]
    down_ref[6] = columns_ref[:8, :]


U_ROWS = ((0, False, 0), (1, False, 1), (6, True, 0), (7, True, 1))
P_ROWS = tuple(((0, False, 2 + d), (6, True, 2 + d), (7, True, 5 + d)) for d in range(3))
F_ROWS = ((0, False, 5), (7, True, 8))
HALO_ROWS = (U_ROWS, *P_ROWS, F_ROWS)


def store_halo_tile(out_ref, field, x, below_ref, above_ref):
    out_ref[...] = jnp.zeros((8, LANES), jnp.float32)
    for row, from_below, tile in HALO_ROWS[field]:
        source = below_ref if from_below else above_ref
        out_ref[row : row + 1, :] = source[tile, x : x + 1, :]


def columns_halo(below_ref, above_ref):
    row = rows_of(8)
    return jnp.where(row >= 6, below_ref[9], jnp.where(row < 2, above_ref[6], 0.0))


def x_faces(u_ref, f_ref, p_ref, columns_ref, below_ref, above_ref, up_ref, down_ref):
    named = fields(u_ref, p_ref, f_ref)
    up = ((0, 6), (0, 7), (1, 6), (2, 6), (3, 6), (1, 7), (2, 7), (3, 7), (4, 7))
    down = ((0, 0), (0, 1), (1, 0), (2, 0), (3, 0), (4, 0))
    for out_ref, planes in ((up_ref, up), (down_ref, down)):
        for k, (field, x) in enumerate(planes):
            out_ref[k, :ROWS, :] = named[field][x]
            store_halo_tile(out_ref.at[k, ROWS:, :], field, x, below_ref, above_ref)
    halo = columns_halo(below_ref, above_ref)
    for out_ref, k in ((up_ref, 9), (down_ref, 6)):
        out_ref[k, :ROWS, :] = columns_ref[...]
        out_ref[k, ROWS:, :] = halo


def y_halo(below_ref, above_ref, out_ref):
    for field in range(5):
        for x in range(OWN):
            store_halo_tile(out_ref.at[field, x], field, x, below_ref, above_ref)


def iterate(
    u_ref, f_ref, p_ref, halo_ref, columns_ref, below_y_ref, above_y_ref, below_ref, above_ref,
    u_out, p_out, sums_out, bar_s, dual_s, primal_s,
):
    size_x = OWN * lax.axis_size(GX)
    size_y = ROWS * lax.axis_size(GY)
    start_x = lax.axis_index(GX) * OWN
    start_y = lax.axis_index(GY) * ROWS
    second = lax.axis_index(GZ)
    later = second.astype(jnp.float32)
    lane = lanes_of(ALL_ROWS)
    row = rows_of(ALL_ROWS)
    odd = (lane & 1) == 1
    last_lane = lane == LANES - 1
    first_lane = lane == 0

    def as_float(mask):
        return jnp.where(mask, 1.0, 0.0)

    place_y = start_y + jnp.where(row < ROWS + 4, row, row - ALL_ROWS)
    inside_y = as_float((place_y >= 0) & (place_y <= size_y - 2))
    inside_z = 1.0 - later * as_float(last_lane)
    place_x = start_x + ((lane % GROUP) >> 1) - 2
    inside_h = as_float((place_x >= 0) & (place_x <= size_x - 2))

    def inside_x(x):
        place = start_x + x
        return jnp.where((place >= 0) & (place <= size_x - 2), 1.0, 0.0)

    def next_row(v):
        return pltpu.roll(v, ALL_ROWS - 1, 0)

    def previous_row(v):
        return pltpu.roll(v, 1, 0)

    def turn(v, by):
        return pltpu.roll(v, by % LANES, 1)

    own_columns = jnp.concatenate([columns_ref[...], columns_halo(below_y_ref, above_y_ref)], axis=0)
    in_group = lane % GROUP
    columns = jnp.where(
        in_group < 4,
        turn(below_ref[9], -16),
        jnp.where(in_group >= 20, turn(above_ref[6], 16), own_columns),
    )
    columns_u, columns_p0, columns_p1, columns_p2, columns_f = [
        turn(columns, -GROUP * g) for g in range(5)
    ]
    columns_p = (columns_p0, columns_p1, columns_p2)

    def plane(field, x):
        if 0 <= x < OWN:
            source = fields(u_ref, p_ref, f_ref)[field]
            return jnp.concatenate([source[x], halo_ref[field, x]], axis=0)
        if x < 0:
            at = {(0, -2): 0, (0, -1): 1, (4, -1): 8}
            at |= {(1 + d, -2): 2 + d for d in range(3)} | {(1 + d, -1): 5 + d for d in range(3)}
            return below_ref[at[field, x]]
        at = {(0, 8): 0, (0, 9): 1, (4, 8): 5} | {(1 + d, 8): 2 + d for d in range(3)}
        return above_ref[at[field, x]]

    def from_columns(v, x):
        return turn(v, LANES - 1 - 2 * (x + 2))

    def into_columns(into, v, x):
        return jnp.where((lane >> 1) == x + 2, turn(v, 2 * (x + 2) + 1), into)

    def project(dual, gradient, inside):
        moved = [p + (STEP_DUAL * i) * g for p, g, i in zip(dual, gradient, inside)]
        square = moved[0] * moved[0] + moved[1] * moved[1] + moved[2] * moved[2]
        scale = RADIUS * lax.rsqrt(jnp.maximum(square, RADIUS * RADIUS))
        return [q * (scale * i) for q, i in zip(moved, inside)]

    def update(u, f, divergence):
        return (u + STEP_PRIMAL * (divergence + f)) * (1.0 / (1.0 + STEP_PRIMAL))

    def fold(v):
        return v[0:8] + v[8:16] + v[16:24] + v[24:32]

    one = jnp.ones((ALL_ROWS, LANES), jnp.float32)
    totals = []
    for turn_k in range(2):
        low, high = ((-2, 9), (-1, 8))[turn_k]

        def bar(x):
            return plane(0, x) if turn_k == 0 else bar_s[x + 2]

        def dual(x):
            if turn_k == 0:
                return [plane(1 + d, x) for d in range(3)]
            return [dual_s[d, x + 2] for d in range(3)]

        def current(x):
            return plane(0, x) if turn_k == 0 else primal_s[x + 2]

        if turn_k == 0:
            columns_bar = columns_u
        gathered = jnp.zeros((ALL_ROWS, LANES), jnp.float32)
        for x in range(low, high):
            gathered = into_columns(gathered, bar(x), x)
        columns_gradient = (
            turn(columns_bar, -2) - columns_bar,
            next_row(columns_bar) - columns_bar,
            jnp.where(odd, gathered, turn(columns_bar, -1)) - columns_bar,
        )
        columns_new = project(columns_p, columns_gradient, (inside_h, inside_y, one))

        total = jnp.zeros((8, LANES), jnp.float32)
        gathered = jnp.zeros((ALL_ROWS, LANES), jnp.float32)
        previous = None
        for x in range(low, high):
            here = bar(x)
            old = dual(x)
            following = jnp.where(last_lane, from_columns(columns_bar, x), turn(here, -1))
            gradient = (bar(x + 1) - here, next_row(here) - here, following - here)
            new = project(old, gradient, (inside_x(x), inside_y, inside_z))
            if 0 <= x < OWN:
                change = sum((n - o) * (n - o) for n, o in zip(new, old))
                total += fold(change) * (1.0 / STEP_DUAL)
            gathered = into_columns(gathered, new[2], x)

            if x > low:
                before = jnp.where(
                    first_lane, later * from_columns(columns_new[2], x), turn(new[2], 1)
                )
                divergence = (
                    new[0] - previous + new[1] - previous_row(new[1]) + new[2] - before
                )
                now = current(x)
                updated = update(now, plane(4, x), divergence)
                if 0 <= x < OWN:
                    change = updated - now
                    total += fold(change * change) * (1.0 / STEP_PRIMAL)
                if turn_k == 0:
                    bar_s[x + 2] = 2.0 * updated - now
                    primal_s[x + 2] = updated
                    for d in range(3):
                        dual_s[d, x + 2] = new[d]
                else:
                    u_out[x] = updated[:ROWS]
                    for d in range(3):
                        p_out[d, x] = new[d][:ROWS]
            previous = new[0]
        totals.append(jnp.sum(total))

        if turn_k == 0:
            divergence = (
                columns_new[0] - turn(columns_new[0], 2)
                + columns_new[1] - previous_row(columns_new[1])
                + columns_new[2] - jnp.where(odd, turn(columns_new[2], 1), gathered)
            )
            updated = update(columns_u, columns_f, divergence)
            columns_bar = 2.0 * updated - columns_u
            columns_p = columns_new
    out_lane = lanes_of(8)
    sums_out[...] = jnp.where(out_lane == 0, totals[0], jnp.where(out_lane == 1, totals[1], 0.0))


def shape(*dims):
    return jax.ShapeDtypeStruct(dims, jnp.float32)


def call(kernel, count, outs, scratch=(), flops=0, size=0):
    return pl.pallas_call(
        kernel,
        out_shape=outs,
        in_specs=[VMEM] * count,
        out_specs=jax.tree.map(lambda _: VMEM, outs),
        scratch_shapes=list(scratch),
        cost_estimate=pl.CostEstimate(flops=flops, bytes_accessed=size, transcendentals=0),
    )


def shifted(axes, by):
    count = lax.axis_size(axes)
    return [(i, (i + by) % count) for i in range(count)]


def settle(values):
    for axes in (("xl", "core", "xh"), ("z", "y")):
        count = lax.axis_size(axes)
        spread = jnp.broadcast_to(values[:1, :2], (count, 2))
        values = jnp.sum(lax.all_to_all(spread, axes, 0, 0, tiled=True), axis=0, keepdims=True)
    return values[0, :2]


def on_device(f, u, p):
    columns = call(z_faces, 3, shape(ROWS, LANES))(u, f, p)
    columns = lax.ppermute(columns, GZ, shifted(GZ, 1))

    up, down = call(y_faces, 4, (shape(10, 8, LANES), shape(7, 8, LANES)))(u, f, p, columns)
    below_y = lax.ppermute(up, GY, shifted(GY, 1))
    above_y = lax.ppermute(down, GY, shifted(GY, -1))

    faces = (shape(10, ALL_ROWS, LANES), shape(7, ALL_ROWS, LANES))
    up, down = call(x_faces, 6, faces)(u, f, p, columns, below_y, above_y)
    below = lax.ppermute(up, GX, shifted(GX, 1))
    above = lax.ppermute(down, GX, shifted(GX, -1))

    halo = call(y_halo, 2, shape(5, OWN, 8, LANES))(below_y, above_y)
    denoised, dual, sums = call(
        iterate,
        9,
        (shape(OWN, ROWS, LANES), shape(3, OWN, ROWS, LANES), shape(8, LANES)),
        (
            pltpu.VMEM((12, ALL_ROWS, LANES), jnp.float32),
            pltpu.VMEM((3, 12, ALL_ROWS, LANES), jnp.float32),
            pltpu.VMEM((12, ALL_ROWS, LANES), jnp.float32),
        ),
    )(u, f, p, halo, columns, below_y, above_y, below, above)
    cells = OWN * lax.axis_size(GX) * ROWS * lax.axis_size(GY) * LANES * lax.axis_size(GZ)
    return denoised, dual, jnp.sqrt(settle(sums) / float(cells))


def solution(mesh):
    mesh = Mesh(mesh.devices.reshape(SIZES), ("xl", "z", "core", "y", "xh"))
    placed = (P(GX, GY, GZ), P(GX, GY, GZ), P(None, GX, GY, GZ))
    return jax.shard_map(
        on_device,
        mesh=mesh,
        in_specs=placed,
        out_specs=(P(GX, GY, GZ), P(None, GX, GY, GZ), P()),
        check_vma=False,
    )
```

```python
import jax
import jax.numpy as jnp
from jax import lax
from jax.experimental import pallas as pl
from jax.experimental.pallas import tpu as pltpu
from jax.sharding import Mesh, PartitionSpec as P


GX = ("xl", "z", "core")
GY = "y"
GZ = "xh"
SIZES = (2, 8, 2, 8, 2)

STEP_PRIMAL = 0.25
STEP_DUAL = 0.3
RADIUS = 0.5
OWN = 8
ROWS = 32
ALL_ROWS = 40
LANES = 128
GROUP = 24

VMEM = pl.BlockSpec(memory_space=pltpu.VMEM)


def lanes_of(rows):
    return lax.broadcasted_iota(jnp.int32, (rows, LANES), 1)


def rows_of(rows):
    return lax.broadcasted_iota(jnp.int32, (rows, LANES), 0)


def fields(u_ref, p_ref, f_ref):
    return (u_ref, p_ref.at[0], p_ref.at[1], p_ref.at[2], f_ref)


def z_faces(u_ref, f_ref, p_ref, out_ref):
    first = 1 - lax.axis_index(GZ)
    pair = lanes_of(ROWS) >> 1
    columns = jnp.zeros((ROWS, LANES), jnp.float32)
    for g, field in enumerate(fields(u_ref, p_ref, f_ref)):
        for x in range(OWN):
            lane = g * GROUP + 2 * (x + 2)
            moved = pltpu.roll(field[x], lane + 2 * first, 1)
            columns = jnp.where(pair == lane // 2, moved, columns)
    out_ref[...] = columns


def y_faces(u_ref, f_ref, p_ref, columns_ref, up_ref, down_ref):
    up_ref[0] = u_ref[:, ROWS - 2, :]
    up_ref[1] = u_ref[:, ROWS - 1, :]
    down_ref[0] = u_ref[:, 0, :]
    down_ref[1] = u_ref[:, 1, :]
    for d in range(3):
        up_ref[2 + d] = p_ref[d, :, ROWS - 2, :]
        up_ref[5 + d] = p_ref[d, :, ROWS - 1, :]
        down_ref[2 + d] = p_ref[d, :, 0, :]
    up_ref[8] = f_ref[:, ROWS - 1, :]
    down_ref[5] = f_ref[:, 0, :]
    up_ref[9] = columns_ref[ROWS - 8 :, :]
    down_ref[6] = columns_ref[:8, :]


U_ROWS = ((0, False, 0), (1, False, 1), (6, True, 0), (7, True, 1))
P_ROWS = tuple(((0, False, 2 + d), (6, True, 2 + d), (7, True, 5 + d)) for d in range(3))
F_ROWS = ((0, False, 5), (7, True, 8))
HALO_ROWS = (U_ROWS, *P_ROWS, F_ROWS)


def store_halo_tile(out_ref, field, x, below_ref, above_ref):
    out_ref[...] = jnp.zeros((8, LANES), jnp.float32)
    for row, from_below, tile in HALO_ROWS[field]:
        source = below_ref if from_below else above_ref
        out_ref[row : row + 1, :] = source[tile, x : x + 1, :]


def columns_halo(below_ref, above_ref):
    row = rows_of(8)
    return jnp.where(row >= 6, below_ref[9], jnp.where(row < 2, above_ref[6], 0.0))


def x_faces(u_ref, f_ref, p_ref, columns_ref, below_ref, above_ref, up_ref, down_ref):
    named = fields(u_ref, p_ref, f_ref)
    up = ((0, 6), (0, 7), (1, 6), (2, 6), (3, 6), (1, 7), (2, 7), (3, 7), (4, 7))
    down = ((0, 0), (0, 1), (1, 0), (2, 0), (3, 0), (4, 0))
    for out_ref, planes in ((up_ref, up), (down_ref, down)):
        for k, (field, x) in enumerate(planes):
            out_ref[k, :ROWS, :] = named[field][x]
            store_halo_tile(out_ref.at[k, ROWS:, :], field, x, below_ref, above_ref)
    halo = columns_halo(below_ref, above_ref)
    for out_ref, k in ((up_ref, 9), (down_ref, 6)):
        out_ref[k, :ROWS, :] = columns_ref[...]
        out_ref[k, ROWS:, :] = halo


def y_halo(below_ref, above_ref, out_ref):
    for field in range(5):
        for x in range(OWN):
            store_halo_tile(out_ref.at[field, x], field, x, below_ref, above_ref)


def iterate(
    u_ref, f_ref, p_ref, halo_ref, columns_ref, below_y_ref, above_y_ref, below_ref, above_ref,
    u_out, p_out, sums_out, bar_s, dual_s, primal_s,
):
    size_x = OWN * lax.axis_size(GX)
    size_y = ROWS * lax.axis_size(GY)
    start_x = lax.axis_index(GX) * OWN
    start_y = lax.axis_index(GY) * ROWS
    second = lax.axis_index(GZ)
    later = second.astype(jnp.float32)
    lane = lanes_of(ALL_ROWS)
    row = rows_of(ALL_ROWS)
    odd = (lane & 1) == 1
    last_lane = lane == LANES - 1
    first_lane = lane == 0

    def as_float(mask):
        return jnp.where(mask, 1.0, 0.0)

    place_y = start_y + jnp.where(row < ROWS + 4, row, row - ALL_ROWS)
    inside_y = as_float((place_y >= 0) & (place_y <= size_y - 2))
    inside_z = 1.0 - later * as_float(last_lane)
    place_x = start_x + ((lane % GROUP) >> 1) - 2
    inside_h = as_float((place_x >= 0) & (place_x <= size_x - 2))

    def inside_x(x):
        place = start_x + x
        return jnp.where((place >= 0) & (place <= size_x - 2), 1.0, 0.0)

    def next_row(v):
        return pltpu.roll(v, ALL_ROWS - 1, 0)

    def previous_row(v):
        return pltpu.roll(v, 1, 0)

    def turn(v, by):
        return pltpu.roll(v, by % LANES, 1)

    own_columns = jnp.concatenate([columns_ref[...], columns_halo(below_y_ref, above_y_ref)], axis=0)
    in_group = lane % GROUP
    columns = jnp.where(
        in_group < 4,
        turn(below_ref[9], -16),
        jnp.where(in_group >= 20, turn(above_ref[6], 16), own_columns),
    )
    columns_u, columns_p0, columns_p1, columns_p2, columns_f = [
        turn(columns, -GROUP * g) for g in range(5)
    ]
    columns_p = (columns_p0, columns_p1, columns_p2)

    def plane(field, x):
        if 0 <= x < OWN:
            source = fields(u_ref, p_ref, f_ref)[field]
            return jnp.concatenate([source[x], halo_ref[field, x]], axis=0)
        if x < 0:
            at = {(0, -2): 0, (0, -1): 1, (4, -1): 8}
            at |= {(1 + d, -2): 2 + d for d in range(3)} | {(1 + d, -1): 5 + d for d in range(3)}
            return below_ref[at[field, x]]
        at = {(0, 8): 0, (0, 9): 1, (4, 8): 5} | {(1 + d, 8): 2 + d for d in range(3)}
        return above_ref[at[field, x]]

    def from_columns(v, x):
        return turn(v, LANES - 1 - 2 * (x + 2))

    def into_columns(into, v, x):
        return jnp.where((lane >> 1) == x + 2, turn(v, 2 * (x + 2) + 1), into)

    def project(dual, gradient, inside):
        moved = [p + (STEP_DUAL * i) * g for p, g, i in zip(dual, gradient, inside)]
        square = moved[0] * moved[0] + moved[1] * moved[1] + moved[2] * moved[2]
        scale = RADIUS * lax.rsqrt(jnp.maximum(square, RADIUS * RADIUS))
        return [q * (scale * i) for q, i in zip(moved, inside)]

    def update(u, f, divergence):
        return (u + STEP_PRIMAL * (divergence + f)) * (1.0 / (1.0 + STEP_PRIMAL))

    def fold(v):
        return v[0:8] + v[8:16] + v[16:24] + v[24:32]

    one = jnp.ones((ALL_ROWS, LANES), jnp.float32)
    totals = []
    for turn_k in range(2):
        low, high = ((-2, 9), (-1, 8))[turn_k]

        def bar(x):
            return plane(0, x) if turn_k == 0 else bar_s[x + 2]

        def dual(x):
            if turn_k == 0:
                return [plane(1 + d, x) for d in range(3)]
            return [dual_s[d, x + 2] for d in range(3)]

        def current(x):
            return plane(0, x) if turn_k == 0 else primal_s[x + 2]

        if turn_k == 0:
            columns_bar = columns_u
        gathered = jnp.zeros((ALL_ROWS, LANES), jnp.float32)
        for x in range(low, high):
            gathered = into_columns(gathered, bar(x), x)
        columns_gradient = (
            turn(columns_bar, -2) - columns_bar,
            next_row(columns_bar) - columns_bar,
            jnp.where(odd, gathered, turn(columns_bar, -1)) - columns_bar,
        )
        columns_new = project(columns_p, columns_gradient, (inside_h, inside_y, one))

        total = jnp.zeros((8, LANES), jnp.float32)
        gathered = jnp.zeros((ALL_ROWS, LANES), jnp.float32)
        previous = None
        for x in range(low, high):
            here = bar(x)
            old = dual(x)
            following = jnp.where(last_lane, from_columns(columns_bar, x), turn(here, -1))
            gradient = (bar(x + 1) - here, next_row(here) - here, following - here)
            new = project(old, gradient, (inside_x(x), inside_y, inside_z))
            if 0 <= x < OWN:
                change = sum((n - o) * (n - o) for n, o in zip(new, old))
                total += fold(change) * (1.0 / STEP_DUAL)
            gathered = into_columns(gathered, new[2], x)

            if x > low:
                before = jnp.where(
                    first_lane, later * from_columns(columns_new[2], x), turn(new[2], 1)
                )
                divergence = (
                    new[0] - previous + new[1] - previous_row(new[1]) + new[2] - before
                )
                now = current(x)
                updated = update(now, plane(4, x), divergence)
                if 0 <= x < OWN:
                    change = updated - now
                    total += fold(change * change) * (1.0 / STEP_PRIMAL)
                if turn_k == 0:
                    bar_s[x + 2] = 2.0 * updated - now
                    primal_s[x + 2] = updated
                    for d in range(3):
                        dual_s[d, x + 2] = new[d]
                else:
                    u_out[x] = updated[:ROWS]
                    for d in range(3):
                        p_out[d, x] = new[d][:ROWS]
            previous = new[0]
        totals.append(jnp.sum(total))

        if turn_k == 0:
            divergence = (
                columns_new[0] - turn(columns_new[0], 2)
                + columns_new[1] - previous_row(columns_new[1])
                + columns_new[2] - jnp.where(odd, turn(columns_new[2], 1), gathered)
            )
            updated = update(columns_u, columns_f, divergence)
            columns_bar = 2.0 * updated - columns_u
            columns_p = columns_new
    out_lane = lanes_of(8)
    sums_out[...] = jnp.where(out_lane == 0, totals[0], jnp.where(out_lane == 1, totals[1], 0.0))


def shape(*dims):
    return jax.ShapeDtypeStruct(dims, jnp.float32)


def call(kernel, count, outs, scratch=(), limit=4):
    return pl.pallas_call(
        kernel,
        out_shape=outs,
        in_specs=[VMEM] * count,
        out_specs=jax.tree.map(lambda _: VMEM, outs),
        scratch_shapes=list(scratch),
        compiler_params=pltpu.CompilerParams(vmem_limit_bytes=limit * 2**20),
    )


def shifted(axes, by):
    count = lax.axis_size(axes)
    return [(i, (i + by) % count) for i in range(count)]


def settle(values):
    for axes in (("xl", "core", "xh"), ("z", "y")):
        count = lax.axis_size(axes)
        spread = jnp.broadcast_to(values[:1, :2], (count, 2))
        values = jnp.sum(lax.all_to_all(spread, axes, 0, 0, tiled=True), axis=0, keepdims=True)
    return values[0, :2]


def on_device(f, u, p):
    columns = call(z_faces, 3, shape(ROWS, LANES))(u, f, p)
    columns = lax.ppermute(columns, GZ, shifted(GZ, 1))

    up, down = call(y_faces, 4, (shape(10, 8, LANES), shape(7, 8, LANES)))(u, f, p, columns)
    below_y = lax.ppermute(up, GY, shifted(GY, 1))
    above_y = lax.ppermute(down, GY, shifted(GY, -1))

    faces = (shape(10, ALL_ROWS, LANES), shape(7, ALL_ROWS, LANES))
    up, down = call(x_faces, 6, faces)(u, f, p, columns, below_y, above_y)
    below = lax.ppermute(up, GX, shifted(GX, 1))
    above = lax.ppermute(down, GX, shifted(GX, -1))

    halo = call(y_halo, 2, shape(5, OWN, 8, LANES))(below_y, above_y)
    denoised, dual, sums = call(
        iterate,
        9,
        (shape(OWN, ROWS, LANES), shape(3, OWN, ROWS, LANES), shape(8, LANES)),
        (
            pltpu.VMEM((12, ALL_ROWS, LANES), jnp.float32),
            pltpu.VMEM((3, 12, ALL_ROWS, LANES), jnp.float32),
            pltpu.VMEM((12, ALL_ROWS, LANES), jnp.float32),
        ),
    )(u, f, p, halo, columns, below_y, above_y, below, above)
    cells = OWN * lax.axis_size(GX) * ROWS * lax.axis_size(GY) * LANES * lax.axis_size(GZ)
    return denoised, dual, jnp.sqrt(settle(sums) / float(cells))


def solution(mesh):
    mesh = Mesh(mesh.devices.reshape(SIZES), ("xl", "z", "core", "y", "xh"))
    placed = (P(GX, GY, GZ), P(GX, GY, GZ), P(None, GX, GY, GZ))
    return jax.shard_map(
        on_device,
        mesh=mesh,
        in_specs=placed,
        out_specs=(P(GX, GY, GZ), P(None, GX, GY, GZ), P()),
        check_vma=False,
    )
```

```python
import jax
import jax.numpy as jnp
from jax import lax
from jax.experimental import pallas as pl
from jax.experimental.pallas import tpu as pltpu
from jax.sharding import Mesh, PartitionSpec as P


GX = ("xl", "z", "core")
GY = "y"
GZ = "xh"
SIZES = (2, 8, 2, 8, 2)

STEP_PRIMAL = 0.25
STEP_DUAL = 0.3
RADIUS = 0.5
OWN = 8
ROWS = 32
ALL_ROWS = 40
LANES = 128
GROUP = 24

VMEM = pl.BlockSpec(memory_space=pltpu.VMEM)


def lanes_of(rows):
    return lax.broadcasted_iota(jnp.int32, (rows, LANES), 1)


def rows_of(rows):
    return lax.broadcasted_iota(jnp.int32, (rows, LANES), 0)


def fields(u_ref, p_ref, f_ref):
    return (u_ref, p_ref.at[0], p_ref.at[1], p_ref.at[2], f_ref)


def load(u_ref, f_ref, p_ref, out_ref, u_vmem, f_vmem, p_vmem, sem):
    copies = [
        pltpu.make_async_copy(source, target, sem.at[k])
        for k, (source, target) in enumerate(
            ((u_ref, u_vmem), (f_ref, f_vmem), (p_ref, p_vmem))
        )
    ]
    for copy in copies:
        copy.start()
    for copy in copies:
        copy.wait()
    z_faces(u_vmem, f_vmem, p_vmem, out_ref)


def z_faces(u_ref, f_ref, p_ref, out_ref):
    first = 1 - lax.axis_index(GZ)
    pair = lanes_of(ROWS) >> 1
    columns = jnp.zeros((ROWS, LANES), jnp.float32)
    for g, field in enumerate(fields(u_ref, p_ref, f_ref)):
        for x in range(OWN):
            lane = g * GROUP + 2 * (x + 2)
            moved = pltpu.roll(field[x], lane + 2 * first, 1)
            columns = jnp.where(pair == lane // 2, moved, columns)
    out_ref[...] = columns


def y_faces(u_ref, f_ref, p_ref, columns_ref, up_ref, down_ref):
    up_ref[0] = u_ref[:, ROWS - 2, :]
    up_ref[1] = u_ref[:, ROWS - 1, :]
    down_ref[0] = u_ref[:, 0, :]
    down_ref[1] = u_ref[:, 1, :]
    for d in range(3):
        up_ref[2 + d] = p_ref[d, :, ROWS - 2, :]
        up_ref[5 + d] = p_ref[d, :, ROWS - 1, :]
        down_ref[2 + d] = p_ref[d, :, 0, :]
    up_ref[8] = f_ref[:, ROWS - 1, :]
    down_ref[5] = f_ref[:, 0, :]
    up_ref[9] = columns_ref[ROWS - 8 :, :]
    down_ref[6] = columns_ref[:8, :]


U_ROWS = ((0, False, 0), (1, False, 1), (6, True, 0), (7, True, 1))
P_ROWS = tuple(((0, False, 2 + d), (6, True, 2 + d), (7, True, 5 + d)) for d in range(3))
F_ROWS = ((0, False, 5), (7, True, 8))
HALO_ROWS = (U_ROWS, *P_ROWS, F_ROWS)


def store_halo_tile(out_ref, field, x, below_ref, above_ref):
    out_ref[...] = jnp.zeros((8, LANES), jnp.float32)
    for row, from_below, tile in HALO_ROWS[field]:
        source = below_ref if from_below else above_ref
        out_ref[row : row + 1, :] = source[tile, x : x + 1, :]


def columns_halo(below_ref, above_ref):
    row = rows_of(8)
    return jnp.where(row >= 6, below_ref[9], jnp.where(row < 2, above_ref[6], 0.0))


def x_faces(u_ref, f_ref, p_ref, columns_ref, below_ref, above_ref, up_ref, down_ref):
    named = fields(u_ref, p_ref, f_ref)
    up = ((0, 6), (0, 7), (1, 6), (2, 6), (3, 6), (1, 7), (2, 7), (3, 7), (4, 7))
    down = ((0, 0), (0, 1), (1, 0), (2, 0), (3, 0), (4, 0))
    for out_ref, planes in ((up_ref, up), (down_ref, down)):
        for k, (field, x) in enumerate(planes):
            out_ref[k, :ROWS, :] = named[field][x]
            store_halo_tile(out_ref.at[k, ROWS:, :], field, x, below_ref, above_ref)
    halo = columns_halo(below_ref, above_ref)
    for out_ref, k in ((up_ref, 9), (down_ref, 6)):
        out_ref[k, :ROWS, :] = columns_ref[...]
        out_ref[k, ROWS:, :] = halo


def y_halo(below_ref, above_ref, out_ref):
    for field in range(5):
        for x in range(OWN):
            store_halo_tile(out_ref.at[field, x], field, x, below_ref, above_ref)


def iterate(
    u_ref, f_ref, p_ref, halo_ref, columns_ref, below_y_ref, above_y_ref, below_ref, above_ref,
    u_out, p_out, sums_out, bar_s, dual_s, primal_s,
):
    size_x = OWN * lax.axis_size(GX)
    size_y = ROWS * lax.axis_size(GY)
    start_x = lax.axis_index(GX) * OWN
    start_y = lax.axis_index(GY) * ROWS
    second = lax.axis_index(GZ)
    later = second.astype(jnp.float32)
    lane = lanes_of(ALL_ROWS)
    row = rows_of(ALL_ROWS)
    odd = (lane & 1) == 1
    last_lane = lane == LANES - 1
    first_lane = lane == 0

    def as_float(mask):
        return jnp.where(mask, 1.0, 0.0)

    place_y = start_y + jnp.where(row < ROWS + 4, row, row - ALL_ROWS)
    inside_y = as_float((place_y >= 0) & (place_y <= size_y - 2))
    inside_z = 1.0 - later * as_float(last_lane)
    place_x = start_x + ((lane % GROUP) >> 1) - 2
    inside_h = as_float((place_x >= 0) & (place_x <= size_x - 2))

    def inside_x(x):
        place = start_x + x
        return jnp.where((place >= 0) & (place <= size_x - 2), 1.0, 0.0)

    def next_row(v):
        return pltpu.roll(v, ALL_ROWS - 1, 0)

    def previous_row(v):
        return pltpu.roll(v, 1, 0)

    def turn(v, by):
        return pltpu.roll(v, by % LANES, 1)

    own_columns = jnp.concatenate([columns_ref[...], columns_halo(below_y_ref, above_y_ref)], axis=0)
    in_group = lane % GROUP
    columns = jnp.where(
        in_group < 4,
        turn(below_ref[9], -16),
        jnp.where(in_group >= 20, turn(above_ref[6], 16), own_columns),
    )
    columns_u, columns_p0, columns_p1, columns_p2, columns_f = [
        turn(columns, -GROUP * g) for g in range(5)
    ]
    columns_p = (columns_p0, columns_p1, columns_p2)

    def plane(field, x):
        if 0 <= x < OWN:
            source = fields(u_ref, p_ref, f_ref)[field]
            return jnp.concatenate([source[x], halo_ref[field, x]], axis=0)
        if x < 0:
            at = {(0, -2): 0, (0, -1): 1, (4, -1): 8}
            at |= {(1 + d, -2): 2 + d for d in range(3)} | {(1 + d, -1): 5 + d for d in range(3)}
            return below_ref[at[field, x]]
        at = {(0, 8): 0, (0, 9): 1, (4, 8): 5} | {(1 + d, 8): 2 + d for d in range(3)}
        return above_ref[at[field, x]]

    def from_columns(v, x):
        return turn(v, LANES - 1 - 2 * (x + 2))

    def into_columns(into, v, x):
        return jnp.where((lane >> 1) == x + 2, turn(v, 2 * (x + 2) + 1), into)

    def project(dual, gradient, inside):
        moved = [p + (STEP_DUAL * i) * g for p, g, i in zip(dual, gradient, inside)]
        square = moved[0] * moved[0] + moved[1] * moved[1] + moved[2] * moved[2]
        scale = RADIUS * lax.rsqrt(jnp.maximum(square, RADIUS * RADIUS))
        return [q * (scale * i) for q, i in zip(moved, inside)]

    def update(u, f, divergence):
        return (u + STEP_PRIMAL * (divergence + f)) * (1.0 / (1.0 + STEP_PRIMAL))

    def fold(v):
        return v[0:8] + v[8:16] + v[16:24] + v[24:32]

    one = jnp.ones((ALL_ROWS, LANES), jnp.float32)
    totals = []
    for turn_k in range(2):
        low, high = ((-2, 9), (-1, 8))[turn_k]

        def bar(x):
            return plane(0, x) if turn_k == 0 else bar_s[x + 2]

        def dual(x):
            if turn_k == 0:
                return [plane(1 + d, x) for d in range(3)]
            return [dual_s[d, x + 2] for d in range(3)]

        def current(x):
            return plane(0, x) if turn_k == 0 else primal_s[x + 2]

        if turn_k == 0:
            columns_bar = columns_u
        gathered = jnp.zeros((ALL_ROWS, LANES), jnp.float32)
        for x in range(low, high):
            gathered = into_columns(gathered, bar(x), x)
        columns_gradient = (
            turn(columns_bar, -2) - columns_bar,
            next_row(columns_bar) - columns_bar,
            jnp.where(odd, gathered, turn(columns_bar, -1)) - columns_bar,
        )
        columns_new = project(columns_p, columns_gradient, (inside_h, inside_y, one))

        total = jnp.zeros((8, LANES), jnp.float32)
        gathered = jnp.zeros((ALL_ROWS, LANES), jnp.float32)
        previous = None
        for x in range(low, high):
            here = bar(x)
            old = dual(x)
            following = jnp.where(last_lane, from_columns(columns_bar, x), turn(here, -1))
            gradient = (bar(x + 1) - here, next_row(here) - here, following - here)
            new = project(old, gradient, (inside_x(x), inside_y, inside_z))
            if 0 <= x < OWN:
                change = sum((n - o) * (n - o) for n, o in zip(new, old))
                total += fold(change) * (1.0 / STEP_DUAL)
            gathered = into_columns(gathered, new[2], x)

            if x > low:
                before = jnp.where(
                    first_lane, later * from_columns(columns_new[2], x), turn(new[2], 1)
                )
                divergence = (
                    new[0] - previous + new[1] - previous_row(new[1]) + new[2] - before
                )
                now = current(x)
                updated = update(now, plane(4, x), divergence)
                if 0 <= x < OWN:
                    change = updated - now
                    total += fold(change * change) * (1.0 / STEP_PRIMAL)
                if turn_k == 0:
                    bar_s[x + 2] = 2.0 * updated - now
                    primal_s[x + 2] = updated
                    for d in range(3):
                        dual_s[d, x + 2] = new[d]
                else:
                    u_out[x] = updated[:ROWS]
                    for d in range(3):
                        p_out[d, x] = new[d][:ROWS]
            previous = new[0]
        totals.append(jnp.sum(total))

        if turn_k == 0:
            divergence = (
                columns_new[0] - turn(columns_new[0], 2)
                + columns_new[1] - previous_row(columns_new[1])
                + columns_new[2] - jnp.where(odd, turn(columns_new[2], 1), gathered)
            )
            updated = update(columns_u, columns_f, divergence)
            columns_bar = 2.0 * updated - columns_u
            columns_p = columns_new
    out_lane = lanes_of(8)
    sums_out[...] = jnp.where(out_lane == 0, totals[0], jnp.where(out_lane == 1, totals[1], 0.0))


def shape(*dims):
    return jax.ShapeDtypeStruct(dims, jnp.float32)


def call(kernel, count, outs, scratch=(), limit=4):
    return pl.pallas_call(
        kernel,
        out_shape=outs,
        in_specs=[VMEM] * count,
        out_specs=jax.tree.map(lambda _: VMEM, outs),
        scratch_shapes=list(scratch),
        compiler_params=pltpu.CompilerParams(vmem_limit_bytes=limit * 2**20),
    )


def shifted(axes, by):
    count = lax.axis_size(axes)
    return [(i, (i + by) % count) for i in range(count)]


def settle(values):
    for axes in (("xl", "core", "xh"), ("z", "y")):
        count = lax.axis_size(axes)
        spread = jnp.broadcast_to(values[:1, :2], (count, 2))
        values = jnp.sum(lax.all_to_all(spread, axes, 0, 0, tiled=True), axis=0, keepdims=True)
    return values[0, :2]


def on_device(f, u, p):
    columns, u, f, p = pl.pallas_call(
        load,
        out_shape=(shape(ROWS, LANES), shape(*u.shape), shape(*f.shape), shape(*p.shape)),
        in_specs=[pl.BlockSpec(memory_space=pltpu.HBM)] * 3,
        out_specs=(VMEM,) * 4,
        scratch_shapes=[pltpu.SemaphoreType.DMA((3,))],
        compiler_params=pltpu.CompilerParams(vmem_limit_bytes=4 * 2**20),
    )(*[pltpu.with_memory_space_constraint(v, pltpu.HBM) for v in (u, f, p)])
    columns = lax.ppermute(columns, GZ, shifted(GZ, 1))

    up, down = call(y_faces, 4, (shape(10, 8, LANES), shape(7, 8, LANES)))(u, f, p, columns)
    below_y = lax.ppermute(up, GY, shifted(GY, 1))
    above_y = lax.ppermute(down, GY, shifted(GY, -1))

    faces = (shape(10, ALL_ROWS, LANES), shape(7, ALL_ROWS, LANES))
    up, down = call(x_faces, 6, faces)(u, f, p, columns, below_y, above_y)
    below = lax.ppermute(up, GX, shifted(GX, 1))
    above = lax.ppermute(down, GX, shifted(GX, -1))

    halo = call(y_halo, 2, shape(5, OWN, 8, LANES))(below_y, above_y)
    denoised, dual, sums = call(
        iterate,
        9,
        (shape(OWN, ROWS, LANES), shape(3, OWN, ROWS, LANES), shape(8, LANES)),
        (
            pltpu.VMEM((12, ALL_ROWS, LANES), jnp.float32),
            pltpu.VMEM((3, 12, ALL_ROWS, LANES), jnp.float32),
            pltpu.VMEM((12, ALL_ROWS, LANES), jnp.float32),
        ),
    )(u, f, p, halo, columns, below_y, above_y, below, above)
    cells = OWN * lax.axis_size(GX) * ROWS * lax.axis_size(GY) * LANES * lax.axis_size(GZ)
    return denoised, dual, jnp.sqrt(settle(sums) / float(cells))


def solution(mesh):
    mesh = Mesh(mesh.devices.reshape(SIZES), ("xl", "z", "core", "y", "xh"))
    placed = (P(GX, GY, GZ), P(GX, GY, GZ), P(None, GX, GY, GZ))
    return jax.shard_map(
        on_device,
        mesh=mesh,
        in_specs=placed,
        out_specs=(P(GX, GY, GZ), P(None, GX, GY, GZ), P()),
        check_vma=False,
    )
```

```python
import jax
import jax.numpy as jnp
from jax import lax
from jax.experimental import pallas as pl
from jax.experimental.pallas import tpu as pltpu
from jax.sharding import Mesh, PartitionSpec as P


GX = ("xl", "z", "core")
GY = "y"
GZ = "xh"
SIZES = (2, 8, 2, 8, 2)

STEP_PRIMAL = 0.25
STEP_DUAL = 0.3
RADIUS = 0.5
OWN = 8
ROWS = 32
ALL_ROWS = 40
LANES = 128
GROUP = 24

VMEM = pl.BlockSpec(memory_space=pltpu.VMEM)


def lanes_of(rows):
    return lax.broadcasted_iota(jnp.int32, (rows, LANES), 1)


def rows_of(rows):
    return lax.broadcasted_iota(jnp.int32, (rows, LANES), 0)


def fields(u_ref, p_ref, f_ref):
    return (u_ref, p_ref.at[0], p_ref.at[1], p_ref.at[2], f_ref)


def next_row(v):
    return pltpu.roll(v, v.shape[0] - 1, 0)


def previous_row(v):
    return pltpu.roll(v, 1, 0)


def turn(v, by):
    return pltpu.roll(v, by % LANES, 1)


def lane_of(x):
    return 2 * (x + 2)


def from_columns(v, x):
    return turn(v, LANES - 1 - lane_of(x))


def into_columns(into, v, x):
    return jnp.where((lanes_of(ALL_ROWS) >> 1) == x + 2, turn(v, lane_of(x) + 1), into)


def load(u_ref, f_ref, p_ref, out_ref, u_vmem, f_vmem, p_vmem, sem):
    copies = [
        pltpu.make_async_copy(source, target, sem.at[k])
        for k, (source, target) in enumerate(
            ((u_ref, u_vmem), (f_ref, f_vmem), (p_ref, p_vmem))
        )
    ]
    for copy in copies:
        copy.start()
    for copy in copies:
        copy.wait()
    first = 1 - lax.axis_index(GZ)
    pair = lanes_of(ROWS) >> 1
    columns = jnp.zeros((ROWS, LANES), jnp.float32)
    for g, field in enumerate(fields(u_vmem, p_vmem, f_vmem)):
        for x in range(OWN):
            lane = g * GROUP + lane_of(x)
            moved = pltpu.roll(field[x], lane + 2 * first, 1)
            columns = jnp.where(pair == lane // 2, moved, columns)
    out_ref[...] = columns


def is_even(axes):
    return lax.rem(lax.axis_index(axes), 2) == 0


def sort_out(even, up, down):
    return jnp.where(even, up, down), jnp.where(even, down, up)


def y_faces(u_ref, f_ref, p_ref, columns_ref, first_ref, second_ref):
    up = [u_ref[:, ROWS - 2, :], u_ref[:, ROWS - 1, :]]
    up += [p_ref[d, :, ROWS - 2, :] for d in range(3)]
    up += [p_ref[d, :, ROWS - 1, :] for d in range(3)]
    up += [f_ref[:, ROWS - 1, :], columns_ref[ROWS - 8 :, :]]
    down = {0: u_ref[:, 0, :], 1: u_ref[:, 1, :], 8: f_ref[:, 0, :], 9: columns_ref[:8, :]}
    down |= {2 + d: p_ref[d, :, 0, :] for d in range(3)}
    even = is_even(GY)
    for k, tile in enumerate(up):
        first_ref[k], second_ref[k] = sort_out(even, tile, down.get(k, tile))


U_ROWS = ((0, False, 0), (1, False, 1), (6, True, 0), (7, True, 1))
P_ROWS = tuple(((0, False, 2 + d), (6, True, 2 + d), (7, True, 5 + d)) for d in range(3))
F_ROWS = ((0, False, 8), (7, True, 8))
HALO_ROWS = (U_ROWS, *P_ROWS, F_ROWS)


class Local:
    def __init__(self):
        self.size_x = OWN * lax.axis_size(GX)
        size_y = ROWS * lax.axis_size(GY)
        self.start_x = lax.axis_index(GX) * OWN
        start_y = lax.axis_index(GY) * ROWS
        self.later = lax.axis_index(GZ).astype(jnp.float32)
        lane = lanes_of(ALL_ROWS)
        row = rows_of(ALL_ROWS)
        self.lane = lane
        self.odd = (lane & 1) == 1
        self.last_lane = lane == LANES - 1
        self.first_lane = lane == 0
        place_y = start_y + jnp.where(row < ROWS + 4, row, row - ALL_ROWS)
        self.inside_y = jnp.where((place_y >= 0) & (place_y <= size_y - 2), 1.0, 0.0)
        self.inside_z = 1.0 - self.later * jnp.where(self.last_lane, 1.0, 0.0)
        place_x = self.start_x + ((lane % GROUP) >> 1) - 2
        self.inside_h = jnp.where((place_x >= 0) & (place_x <= self.size_x - 2), 1.0, 0.0)
        self.columns_inside = (self.inside_h, self.inside_y, 1.0)

    def inside(self, x):
        place = self.start_x + x
        at_x = jnp.where((place >= 0) & (place <= self.size_x - 2), 1.0, 0.0)
        return (at_x, self.inside_y, self.inside_z)

    def columns_at(self, x):
        return (self.lane >> 1) == x + 2

    def following(self, v, columns, x):
        return jnp.where(self.last_lane, from_columns(columns, x), turn(v, -1))

    def preceding(self, v, columns, x):
        return jnp.where(self.first_lane, self.later * from_columns(columns, x), turn(v, 1))

    def columns_following(self, v, gathered):
        return jnp.where(self.odd, gathered, turn(v, -1))

    def columns_preceding(self, v, gathered):
        return jnp.where(self.odd, turn(v, 1), gathered)

    def move(self, dual, bar, nexts, inside):
        return [p + (STEP_DUAL * i) * (n - bar) for p, n, i in zip(dual, nexts, inside)]

    def project(self, moved, inside):
        square = moved[0] * moved[0] + moved[1] * moved[1] + moved[2] * moved[2]
        scale = RADIUS * lax.rsqrt(jnp.maximum(square, RADIUS * RADIUS))
        return [q * (scale * i) for q, i in zip(moved, inside)]

    def dual_plane(self, dual, bar, above, columns_bar, x):
        nexts = (above, next_row(bar), self.following(bar, columns_bar, x))
        inside = self.inside(x)
        return self.project(self.move(dual, bar, nexts, inside), inside)

    def dual_columns(self, dual, bar, gathered):
        moved = self.move(
            dual,
            bar,
            (turn(bar, -2), next_row(bar), self.columns_following(bar, gathered)),
            self.columns_inside,
        )
        return moved, self.project(moved, self.columns_inside)

    def across(self, dual, columns_z, x):
        return dual[1] - previous_row(dual[1]) + dual[2] - self.preceding(dual[2], columns_z, x)

    def columns_across(self, dual, gathered):
        return (
            dual[1] - previous_row(dual[1]) + dual[2] - self.columns_preceding(dual[2], gathered)
        )


UPDATE = 1.0 / (1.0 + STEP_PRIMAL)
BAR_U = 2.0 * UPDATE - 1.0
BAR_F = 2.0 * UPDATE * STEP_PRIMAL


def updated(u, f, divergence):
    return (u + STEP_PRIMAL * (divergence + f)) * UPDATE


def early_bar(u, f):
    return BAR_U * u + BAR_F * f


def fold(v):
    return v[0:8] + v[8:16] + v[16:24] + v[24:32]


def change_of(new, old):
    return sum(fold((n - o) * (n - o)) for n, o in zip(new, old))


def plane_of(u_ref, f_ref, p_ref, halo_ref):
    sources = fields(u_ref, p_ref, f_ref)

    def plane(field, x):
        return jnp.concatenate([sources[field][x], halo_ref[field, x]], axis=0)

    def dual(x):
        return [plane(1 + d, x) for d in range(3)]

    return plane, dual


def split(columns):
    u, p0, p1, p2, f = [turn(columns, -GROUP * g) for g in range(5)]
    return u, [p0, p1, p2], f


def zeros():
    return jnp.zeros((ALL_ROWS, LANES), jnp.float32)


def gather(v, planes):
    into = zeros()
    for x in planes:
        into = into_columns(into, v(x), x)
    return into


def x_faces(
    u_ref, f_ref, p_ref, columns_ref, first_y_ref, second_y_ref,
    halo_ref, columns_out, first_ref, second_ref, below_s, above_s,
):
    even = is_even(GY)
    for k in range(10):
        above_s[k], below_s[k] = sort_out(even, first_y_ref[k], second_y_ref[k])
    for field in range(5):
        for x in range(OWN):
            halo_ref[field, x] = jnp.zeros((8, LANES), jnp.float32)
            for row, from_below, tile in HALO_ROWS[field]:
                source = below_s if from_below else above_s
                halo_ref[field, x, row : row + 1, :] = source[tile, x : x + 1, :]
    row = rows_of(8)
    columns_out[:ROWS, :] = columns_ref[...]
    columns_out[ROWS:, :] = jnp.where(row >= 6, below_s[9], jnp.where(row < 2, above_s[9], 0.0))

    here = Local()
    plane, dual = plane_of(u_ref, f_ref, p_ref, halo_ref)
    c_u, c_p, c_f = split(columns_out[...])
    c_moved, c_dual = here.dual_columns(c_p, c_u, gather(lambda x: plane(0, x), range(OWN)))

    top = OWN - 1
    u, p = plane(0, top), dual(top)
    nexts = (0.0, next_row(u), here.following(u, c_u, top))
    moved = here.move(p, u, nexts, (1.0, here.inside_y, here.inside_z))
    last = here.dual_plane(dual(top - 1), plane(0, top - 1), u, c_u, top - 1)
    up = [*moved, early_bar(u, plane(4, top)) - BAR_F * last[0]]
    c_up = [
        c_p[0] - STEP_DUAL * c_u, c_moved[1], c_moved[2],
        early_bar(c_u, c_f) - BAR_F * turn(c_dual[0], 2),
    ]

    u = plane(0, 0)
    new = here.dual_plane(dual(0), u, plane(0, 1), c_u, 0)
    bar = early_bar(u, plane(4, 0)) + BAR_F * (new[0] + here.across(new, c_dual[2], 0))
    down = [u, bar]
    gathered = into_columns(zeros(), new[2], 0)
    c_bar = early_bar(c_u, c_f) + BAR_F * (c_dual[0] + here.columns_across(c_dual, gathered))
    c_down = [c_u, c_bar]

    def packed(parts):
        group = here.lane // GROUP
        whole = parts[0]
        for k, part in enumerate(parts[1:], 1):
            whole = jnp.where(group == k, turn(part, GROUP * k), whole)
        return whole

    up.append(packed(c_up))
    down = [*down, up[2], up[3], packed(c_down)]
    even = is_even(GX)
    for k in range(5):
        first_ref[k], second_ref[k] = sort_out(even, up[k], down[k])


def early(
    u_ref, f_ref, p_ref, halo_ref, columns_ref,
    dual_out, bar_out, primal_out, dual_end, primal_end, gathered_out, sums_out,
):
    here = Local()
    plane, dual = plane_of(u_ref, f_ref, p_ref, halo_ref)
    c_u, c_p, c_f = split(columns_ref[...])
    sums = [jnp.zeros((8, LANES), jnp.float32) for _ in range(2)]

    gathered_u = gather(lambda x: plane(0, x), range(OWN))
    _, c_dual = here.dual_columns(c_p, c_u, gathered_u)
    gathered_dual = zeros()
    gathered_bar = zeros()
    for x in range(7):
        old = dual(x)
        u = plane(0, x)
        new = here.dual_plane(old, u, plane(0, x + 1), c_u, x)
        sums[0] += change_of(new, old) * (1.0 / STEP_DUAL)
        gathered_dual = into_columns(gathered_dual, new[2], x)
        for d in range(3):
            dual_out[d, x] = new[d]
        if x > 0:
            divergence = new[0] - previous + here.across(new, c_dual[2], x)
            now = updated(u, plane(4, x), divergence)
            bar = 2.0 * now - u
            sums[0] += change_of([now], [u]) * (1.0 / STEP_PRIMAL)
            gathered_bar = into_columns(gathered_bar, bar, x)
            primal_out[x] = now
            bar_out[x] = bar
        previous = new[0]
    divergence = c_dual[0] - turn(c_dual[0], 2) + here.columns_across(c_dual, gathered_dual)
    c_bar = early_bar(c_u, c_f) + BAR_F * divergence

    _, c_end = here.dual_columns(c_dual, c_bar, gathered_bar)
    for x in range(1, 6):
        old = [dual_out[d, x] for d in range(3)]
        new = here.dual_plane(old, bar_out[x], bar_out[x + 1], c_bar, x)
        sums[1] += change_of(new, old) * (1.0 / STEP_DUAL)
        for d in range(3):
            dual_end[d, x] = new[d]
        if x > 1:
            u = primal_out[x]
            divergence = new[0] - previous + here.across(new, c_end[2], x)
            now = updated(u, plane(4, x), divergence)
            sums[1] += change_of([now], [u]) * (1.0 / STEP_PRIMAL)
            primal_end[x] = now[:ROWS]
        previous = new[0]
    for k, v in enumerate((gathered_u, gathered_dual, gathered_bar)):
        gathered_out[k] = v
    for k in range(2):
        sums_out[k] = sums[k]


def late(
    u_ref, f_ref, p_ref, halo_ref, columns_ref, first_x_ref, second_x_ref,
    dual_ref, bar_ref, primal_ref, dual_end, primal_end, gathered_ref, early_sums,
    u_out, p_out, sums_out,
):
    here = Local()
    plane, dual = plane_of(u_ref, f_ref, p_ref, halo_ref)
    even = is_even(GX)
    above, below = zip(*[sort_out(even, first_x_ref[k], second_x_ref[k]) for k in range(5)])
    sums = [early_sums[0], early_sums[1]]

    c_u, c_p, c_f = split(columns_ref[...])
    lowest, highest = here.columns_at(-1), here.columns_at(OWN)

    def from_below(k):
        return turn(below[4], -GROUP * k - 16)

    def from_above(k):
        return turn(above[4], -GROUP * k + 16)

    c_u = jnp.where(highest, from_above(0), c_u)
    c_moved, _ = here.dual_columns(c_p, c_u, gathered_ref[0])
    sent = (from_below(0) + STEP_DUAL * turn(c_u, -2), from_below(1), from_below(2))
    c_moved = [jnp.where(lowest, s, m) for s, m in zip(sent, c_moved)]
    c_dual = here.project(c_moved, here.columns_inside)

    duals = {x: [dual_ref[d, x] for d in range(3)] for x in range(7)}
    bars = {x: bar_ref[x] for x in range(1, 7)}
    primals = {x: primal_ref[x] for x in range(1, 7)}
    top = OWN - 1
    moved = (below[0] + STEP_DUAL * plane(0, 0), below[1], below[2])
    duals[-1] = here.project(moved, here.inside(-1))
    old = dual(top)
    duals[top] = here.dual_plane(old, plane(0, top), above[0], c_u, top)
    sums[0] += change_of(duals[top], old) * (1.0 / STEP_DUAL)
    for x in (0, top):
        u = plane(0, x)
        divergence = duals[x][0] - duals[x - 1][0] + here.across(duals[x], c_dual[2], x)
        primals[x] = updated(u, plane(4, x), divergence)
        bars[x] = 2.0 * primals[x] - u
        sums[0] += change_of([primals[x]], [u]) * (1.0 / STEP_PRIMAL)
    bars[-1] = below[3] + BAR_F * (duals[-1][0] + here.across(duals[-1], c_dual[2], -1))
    bars[OWN] = above[1] - BAR_F * duals[top][0]

    gathered = gathered_ref[1]
    for x in (-1, top):
        gathered = into_columns(gathered, duals[x][2], x)
    known = jnp.where(
        lowest, from_below(3), jnp.where(highest, from_above(1), early_bar(c_u, c_f))
    )
    own_part = jnp.where(highest, 0.0, c_dual[0] + here.columns_across(c_dual, gathered))
    previous = jnp.where(lowest, 0.0, turn(c_dual[0], 2))
    c_bar = known + BAR_F * (own_part - previous)

    gathered = gathered_ref[2]
    for x in (0, top):
        gathered = into_columns(gathered, bars[x], x)
    _, c_end = here.dual_columns(c_dual, c_bar, gathered)
    ends = {x: [dual_end[d, x] for d in range(3)] for x in range(1, 6)}
    for x in (-1, 0, 6, 7):
        ends[x] = here.dual_plane(duals[x], bars[x], bars[x + 1], c_bar, x)
        if x >= 0:
            sums[1] += change_of(ends[x], duals[x]) * (1.0 / STEP_DUAL)
    for x in range(OWN):
        if 2 <= x <= 5:
            u_out[x] = primal_end[x]
        else:
            divergence = ends[x][0] - ends[x - 1][0] + here.across(ends[x], c_end[2], x)
            now = updated(primals[x], plane(4, x), divergence)
            sums[1] += change_of([now], [primals[x]]) * (1.0 / STEP_PRIMAL)
            u_out[x] = now[:ROWS]
        for d in range(3):
            p_out[d, x] = ends[x][d][:ROWS]
    out_lane = lanes_of(8)
    sums_out[...] = jnp.where(
        out_lane == 0, jnp.sum(sums[0]), jnp.where(out_lane == 1, jnp.sum(sums[1]), 0.0)
    )


def shape(*dims):
    return jax.ShapeDtypeStruct(dims, jnp.float32)


def call(kernel, count, outs, scratch=(), specs=None, work=0):
    return pl.pallas_call(
        kernel,
        out_shape=outs,
        in_specs=specs or [VMEM] * count,
        out_specs=jax.tree.map(lambda _: VMEM, outs),
        scratch_shapes=list(scratch),
        compiler_params=pltpu.CompilerParams(vmem_limit_bytes=4 * 2**20),
        cost_estimate=pl.CostEstimate(flops=work, bytes_accessed=work, transcendentals=0),
    )


def trade(first, second, axes):
    count = lax.axis_size(axes)
    outer = [(i, (i + 1 if i % 2 else i - 1) % count) for i in range(count)]
    second = lax.ppermute(second, axes, outer)
    first = lax.ppermute(first, axes, [(i, i ^ 1) for i in range(count)])
    return first, second


def settle(values):
    for axes in (("xl", "core", "xh"), ("z", "y")):
        count = lax.axis_size(axes)
        spread = jnp.broadcast_to(values[:1, :2], (count, 2))
        values = jnp.sum(lax.all_to_all(spread, axes, 0, 0, tiled=True), axis=0, keepdims=True)
    return values[0, :2]


def on_device(f, u, p):
    inputs = [pltpu.with_memory_space_constraint(v, pltpu.HBM) for v in (u, f, p)]
    columns, u, f, p = call(
        load,
        3,
        (shape(ROWS, LANES), shape(*u.shape), shape(*f.shape), shape(*p.shape)),
        [pltpu.SemaphoreType.DMA((3,))],
        [pl.BlockSpec(memory_space=pltpu.HBM)] * 3,
    )(*inputs)
    columns = lax.ppermute(columns, GZ, [(0, 1), (1, 0)])

    message = shape(10, 8, LANES)
    first_y, second_y = trade(*call(y_faces, 4, (message, message))(u, f, p, columns), GY)

    message = shape(5, ALL_ROWS, LANES)
    halo, columns, first, second = call(
        x_faces,
        6,
        (shape(5, OWN, 8, LANES), shape(ALL_ROWS, LANES), message, message),
        [pltpu.VMEM((10, 8, LANES), jnp.float32)] * 2,
    )(u, f, p, columns, first_y, second_y)
    first, second = trade(first, second, GX)

    planes = shape(OWN, ALL_ROWS, LANES)
    triple = shape(3, OWN, ALL_ROWS, LANES)
    done = call(
        early,
        5,
        (
            triple, planes, planes, triple, shape(OWN, ROWS, LANES),
            shape(3, ALL_ROWS, LANES), shape(2, 8, LANES),
        ),
        work=10**6,
    )(u, f, p, halo, columns)
    denoised, dual, sums = call(
        late,
        14,
        (shape(OWN, ROWS, LANES), shape(3, OWN, ROWS, LANES), shape(8, LANES)),
    )(u, f, p, halo, columns, first, second, *done)
    cells = OWN * lax.axis_size(GX) * ROWS * lax.axis_size(GY) * LANES * lax.axis_size(GZ)
    return denoised, dual, jnp.sqrt(settle(sums) / float(cells))


def solution(mesh):
    mesh = Mesh(mesh.devices.reshape(SIZES), ("xl", "z", "core", "y", "xh"))
    placed = (P(GX, GY, GZ), P(GX, GY, GZ), P(None, GX, GY, GZ))
    return jax.shard_map(
        on_device,
        mesh=mesh,
        in_specs=placed,
        out_specs=(P(GX, GY, GZ), P(None, GX, GY, GZ), P()),
        check_vma=False,
    )
```

```python
import jax
import jax.numpy as jnp
from jax import lax
from jax.experimental import pallas as pl
from jax.experimental.pallas import tpu as pltpu
from jax.sharding import Mesh, PartitionSpec as P


GX = ("xl", "z", "core")
GY = "y"
GZ = "xh"
SIZES = (2, 8, 2, 8, 2)

STEP_PRIMAL = 0.25
STEP_DUAL = 0.3
RADIUS = 0.5
OWN = 8
ROWS = 32
ALL_ROWS = 40
LANES = 128
GROUP = 24

VMEM = pl.BlockSpec(memory_space=pltpu.VMEM)


def lanes_of(rows):
    return lax.broadcasted_iota(jnp.int32, (rows, LANES), 1)


def rows_of(rows):
    return lax.broadcasted_iota(jnp.int32, (rows, LANES), 0)


def fields(u_ref, p_ref, f_ref):
    return (u_ref, p_ref.at[0], p_ref.at[1], p_ref.at[2], f_ref)


def next_row(v):
    return pltpu.roll(v, v.shape[0] - 1, 0)


def previous_row(v):
    return pltpu.roll(v, 1, 0)


def turn(v, by):
    return pltpu.roll(v, by % LANES, 1)


def lane_of(x):
    return 2 * (x + 2)


def from_columns(v, x):
    return turn(v, LANES - 1 - lane_of(x))


def into_columns(into, v, x):
    return jnp.where((lanes_of(ALL_ROWS) >> 1) == x + 2, turn(v, lane_of(x) + 1), into)


def load(u_ref, f_ref, p_ref, out_ref, u_vmem, f_vmem, p_vmem, sem):
    copies = [
        pltpu.make_async_copy(source, target, sem.at[k])
        for k, (source, target) in enumerate(
            ((u_ref, u_vmem), (f_ref, f_vmem), (p_ref, p_vmem))
        )
    ]
    for copy in copies:
        copy.start()
    for copy in copies:
        copy.wait()
    first = 1 - lax.axis_index(GZ)
    pair = lanes_of(ROWS) >> 1
    columns = jnp.zeros((ROWS, LANES), jnp.float32)
    for g, field in enumerate(fields(u_vmem, p_vmem, f_vmem)):
        for x in range(OWN):
            lane = g * GROUP + lane_of(x)
            moved = pltpu.roll(field[x], lane + 2 * first, 1)
            columns = jnp.where(pair == lane // 2, moved, columns)
    out_ref[...] = columns


def is_even(axes):
    return lax.rem(lax.axis_index(axes), 2) == 0


def sort_out(even, up, down):
    return jnp.where(even, up, down), jnp.where(even, down, up)


def y_faces(u_ref, f_ref, p_ref, columns_ref, first_ref, second_ref):
    up = [u_ref[:, ROWS - 2, :], u_ref[:, ROWS - 1, :]]
    up += [p_ref[d, :, ROWS - 2, :] for d in range(3)]
    up += [p_ref[d, :, ROWS - 1, :] for d in range(3)]
    up += [f_ref[:, ROWS - 1, :], columns_ref[ROWS - 8 :, :]]
    down = {0: u_ref[:, 0, :], 1: u_ref[:, 1, :], 8: f_ref[:, 0, :], 9: columns_ref[:8, :]}
    down |= {2 + d: p_ref[d, :, 0, :] for d in range(3)}
    even = is_even(GY)
    for k, tile in enumerate(up):
        first_ref[k], second_ref[k] = sort_out(even, tile, down.get(k, tile))


U_ROWS = ((0, False, 0), (1, False, 1), (6, True, 0), (7, True, 1))
P_ROWS = tuple(((0, False, 2 + d), (6, True, 2 + d), (7, True, 5 + d)) for d in range(3))
F_ROWS = ((0, False, 8), (7, True, 8))
HALO_ROWS = (U_ROWS, *P_ROWS, F_ROWS)


class Local:
    def __init__(self):
        self.size_x = OWN * lax.axis_size(GX)
        size_y = ROWS * lax.axis_size(GY)
        self.start_x = lax.axis_index(GX) * OWN
        start_y = lax.axis_index(GY) * ROWS
        self.later = lax.axis_index(GZ).astype(jnp.float32)
        lane = lanes_of(ALL_ROWS)
        row = rows_of(ALL_ROWS)
        self.lane = lane
        self.odd = (lane & 1) == 1
        self.last_lane = lane == LANES - 1
        self.first_lane = lane == 0
        place_y = start_y + jnp.where(row < ROWS + 4, row, row - ALL_ROWS)
        self.inside_y = jnp.where((place_y >= 0) & (place_y <= size_y - 2), 1.0, 0.0)
        self.inside_z = 1.0 - self.later * jnp.where(self.last_lane, 1.0, 0.0)
        place_x = self.start_x + ((lane % GROUP) >> 1) - 2
        self.inside_h = jnp.where((place_x >= 0) & (place_x <= self.size_x - 2), 1.0, 0.0)
        self.columns_inside = (self.inside_h, self.inside_y, 1.0)

    def inside(self, x):
        place = self.start_x + x
        at_x = jnp.where((place >= 0) & (place <= self.size_x - 2), 1.0, 0.0)
        return (at_x, self.inside_y, self.inside_z)

    def columns_at(self, x):
        return (self.lane >> 1) == x + 2

    def following(self, v, columns, x):
        return jnp.where(self.last_lane, from_columns(columns, x), turn(v, -1))

    def preceding(self, v, columns, x):
        return jnp.where(self.first_lane, self.later * from_columns(columns, x), turn(v, 1))

    def columns_following(self, v, gathered):
        return jnp.where(self.odd, gathered, turn(v, -1))

    def columns_preceding(self, v, gathered):
        return jnp.where(self.odd, turn(v, 1), gathered)

    def move(self, dual, bar, nexts, inside):
        return [p + (STEP_DUAL * i) * (n - bar) for p, n, i in zip(dual, nexts, inside)]

    def project(self, moved, inside):
        square = moved[0] * moved[0] + moved[1] * moved[1] + moved[2] * moved[2]
        scale = RADIUS * lax.rsqrt(jnp.maximum(square, RADIUS * RADIUS))
        return [q * (scale * i) for q, i in zip(moved, inside)]

    def dual_plane(self, dual, bar, above, columns_bar, x):
        nexts = (above, next_row(bar), self.following(bar, columns_bar, x))
        inside = self.inside(x)
        return self.project(self.move(dual, bar, nexts, inside), inside)

    def dual_columns(self, dual, bar, gathered):
        moved = self.move(
            dual,
            bar,
            (turn(bar, -2), next_row(bar), self.columns_following(bar, gathered)),
            self.columns_inside,
        )
        return moved, self.project(moved, self.columns_inside)

    def across(self, dual, columns_z, x):
        return dual[1] - previous_row(dual[1]) + dual[2] - self.preceding(dual[2], columns_z, x)

    def columns_across(self, dual, gathered):
        return (
            dual[1] - previous_row(dual[1]) + dual[2] - self.columns_preceding(dual[2], gathered)
        )


UPDATE = 1.0 / (1.0 + STEP_PRIMAL)
BAR_U = 2.0 * UPDATE - 1.0
BAR_F = 2.0 * UPDATE * STEP_PRIMAL


def updated(u, f, divergence):
    return (u + STEP_PRIMAL * (divergence + f)) * UPDATE


def early_bar(u, f):
    return BAR_U * u + BAR_F * f


def fold(v):
    return v[0:8] + v[8:16] + v[16:24] + v[24:32]


def change_of(new, old):
    return sum(fold((n - o) * (n - o)) for n, o in zip(new, old))


def plane_of(u_ref, f_ref, p_ref, halo_ref):
    sources = fields(u_ref, p_ref, f_ref)

    def plane(field, x):
        return jnp.concatenate([sources[field][x], halo_ref[field, x]], axis=0)

    def dual(x):
        return [plane(1 + d, x) for d in range(3)]

    return plane, dual


def split(columns):
    u, p0, p1, p2, f = [turn(columns, -GROUP * g) for g in range(5)]
    return u, [p0, p1, p2], f


def zeros():
    return jnp.zeros((ALL_ROWS, LANES), jnp.float32)


def gather(v, planes):
    into = zeros()
    for x in planes:
        into = into_columns(into, v(x), x)
    return into


def x_faces(
    u_ref, f_ref, p_ref, columns_ref, second_y_ref, first_y_ref,
    halo_ref, columns_out, first_ref, second_ref, below_s, above_s,
):
    even = is_even(GY)
    for k in range(10):
        above_s[k], below_s[k] = sort_out(even, first_y_ref[k], second_y_ref[k])
    for field in range(5):
        for x in range(OWN):
            halo_ref[field, x] = jnp.zeros((8, LANES), jnp.float32)
            for row, from_below, tile in HALO_ROWS[field]:
                source = below_s if from_below else above_s
                halo_ref[field, x, row : row + 1, :] = source[tile, x : x + 1, :]
    row = rows_of(8)
    columns_out[:ROWS, :] = columns_ref[...]
    columns_out[ROWS:, :] = jnp.where(row >= 6, below_s[9], jnp.where(row < 2, above_s[9], 0.0))

    here = Local()
    plane, dual = plane_of(u_ref, f_ref, p_ref, halo_ref)
    c_u, c_p, c_f = split(columns_out[...])
    c_moved, c_dual = here.dual_columns(c_p, c_u, gather(lambda x: plane(0, x), range(OWN)))

    top = OWN - 1
    u, p = plane(0, top), dual(top)
    nexts = (0.0, next_row(u), here.following(u, c_u, top))
    moved = here.move(p, u, nexts, (1.0, here.inside_y, here.inside_z))
    last = here.dual_plane(dual(top - 1), plane(0, top - 1), u, c_u, top - 1)
    up = [*moved, early_bar(u, plane(4, top)) - BAR_F * last[0]]
    c_up = [
        c_p[0] - STEP_DUAL * c_u, c_moved[1], c_moved[2],
        early_bar(c_u, c_f) - BAR_F * turn(c_dual[0], 2),
    ]

    u = plane(0, 0)
    new = here.dual_plane(dual(0), u, plane(0, 1), c_u, 0)
    bar = early_bar(u, plane(4, 0)) + BAR_F * (new[0] + here.across(new, c_dual[2], 0))
    down = [u, bar]
    gathered = into_columns(zeros(), new[2], 0)
    c_bar = early_bar(c_u, c_f) + BAR_F * (c_dual[0] + here.columns_across(c_dual, gathered))
    c_down = [c_u, c_bar]

    def packed(parts):
        group = here.lane // GROUP
        whole = parts[0]
        for k, part in enumerate(parts[1:], 1):
            whole = jnp.where(group == k, turn(part, GROUP * k), whole)
        return whole

    up.append(packed(c_up))
    down = [*down, up[2], up[3], packed(c_down)]
    even = is_even(GX)
    for k in range(5):
        first_ref[k], second_ref[k] = sort_out(even, up[k], down[k])


def early(
    u_ref, f_ref, p_ref, halo_ref, columns_ref,
    dual_out, bar_out, primal_out, dual_end, primal_end, gathered_out, sums_out,
):
    here = Local()
    plane, dual = plane_of(u_ref, f_ref, p_ref, halo_ref)
    c_u, c_p, c_f = split(columns_ref[...])
    sums = [jnp.zeros((8, LANES), jnp.float32) for _ in range(2)]

    gathered_u = gather(lambda x: plane(0, x), range(OWN))
    _, c_dual = here.dual_columns(c_p, c_u, gathered_u)
    gathered_dual = zeros()
    gathered_bar = zeros()
    for x in range(7):
        old = dual(x)
        u = plane(0, x)
        new = here.dual_plane(old, u, plane(0, x + 1), c_u, x)
        sums[0] += change_of(new, old) * (1.0 / STEP_DUAL)
        gathered_dual = into_columns(gathered_dual, new[2], x)
        for d in range(3):
            dual_out[d, x] = new[d]
        if x > 0:
            divergence = new[0] - previous + here.across(new, c_dual[2], x)
            now = updated(u, plane(4, x), divergence)
            bar = 2.0 * now - u
            sums[0] += change_of([now], [u]) * (1.0 / STEP_PRIMAL)
            gathered_bar = into_columns(gathered_bar, bar, x)
            primal_out[x] = now
            bar_out[x] = bar
        previous = new[0]
    divergence = c_dual[0] - turn(c_dual[0], 2) + here.columns_across(c_dual, gathered_dual)
    c_bar = early_bar(c_u, c_f) + BAR_F * divergence

    _, c_end = here.dual_columns(c_dual, c_bar, gathered_bar)
    for x in range(1, 6):
        old = [dual_out[d, x] for d in range(3)]
        new = here.dual_plane(old, bar_out[x], bar_out[x + 1], c_bar, x)
        sums[1] += change_of(new, old) * (1.0 / STEP_DUAL)
        for d in range(3):
            dual_end[d, x] = new[d]
        if x > 1:
            u = primal_out[x]
            divergence = new[0] - previous + here.across(new, c_end[2], x)
            now = updated(u, plane(4, x), divergence)
            sums[1] += change_of([now], [u]) * (1.0 / STEP_PRIMAL)
            primal_end[x] = now[:ROWS]
        previous = new[0]
    for k, v in enumerate((gathered_u, gathered_dual, gathered_bar)):
        gathered_out[k] = v
    for k in range(2):
        sums_out[k] = sums[k]


def late(
    u_ref, f_ref, p_ref, halo_ref, columns_ref, second_x_ref, first_x_ref,
    dual_ref, bar_ref, primal_ref, dual_end, primal_end, gathered_ref, early_sums,
    u_out, p_out, sums_out,
):
    here = Local()
    plane, dual = plane_of(u_ref, f_ref, p_ref, halo_ref)
    even = is_even(GX)
    above, below = zip(*[sort_out(even, first_x_ref[k], second_x_ref[k]) for k in range(5)])
    sums = [early_sums[0], early_sums[1]]

    c_u, c_p, c_f = split(columns_ref[...])
    lowest, highest = here.columns_at(-1), here.columns_at(OWN)

    def from_below(k):
        return turn(below[4], -GROUP * k - 16)

    def from_above(k):
        return turn(above[4], -GROUP * k + 16)

    c_u = jnp.where(highest, from_above(0), c_u)
    c_moved, _ = here.dual_columns(c_p, c_u, gathered_ref[0])
    sent = (from_below(0) + STEP_DUAL * turn(c_u, -2), from_below(1), from_below(2))
    c_moved = [jnp.where(lowest, s, m) for s, m in zip(sent, c_moved)]
    c_dual = here.project(c_moved, here.columns_inside)

    duals = {x: [dual_ref[d, x] for d in range(3)] for x in range(7)}
    bars = {x: bar_ref[x] for x in range(1, 7)}
    primals = {x: primal_ref[x] for x in range(1, 7)}
    top = OWN - 1
    moved = (below[0] + STEP_DUAL * plane(0, 0), below[1], below[2])
    duals[-1] = here.project(moved, here.inside(-1))
    old = dual(top)
    duals[top] = here.dual_plane(old, plane(0, top), above[0], c_u, top)
    sums[0] += change_of(duals[top], old) * (1.0 / STEP_DUAL)
    for x in (0, top):
        u = plane(0, x)
        divergence = duals[x][0] - duals[x - 1][0] + here.across(duals[x], c_dual[2], x)
        primals[x] = updated(u, plane(4, x), divergence)
        bars[x] = 2.0 * primals[x] - u
        sums[0] += change_of([primals[x]], [u]) * (1.0 / STEP_PRIMAL)
    bars[-1] = below[3] + BAR_F * (duals[-1][0] + here.across(duals[-1], c_dual[2], -1))
    bars[OWN] = above[1] - BAR_F * duals[top][0]

    gathered = gathered_ref[1]
    for x in (-1, top):
        gathered = into_columns(gathered, duals[x][2], x)
    known = jnp.where(
        lowest, from_below(3), jnp.where(highest, from_above(1), early_bar(c_u, c_f))
    )
    own_part = jnp.where(highest, 0.0, c_dual[0] + here.columns_across(c_dual, gathered))
    previous = jnp.where(lowest, 0.0, turn(c_dual[0], 2))
    c_bar = known + BAR_F * (own_part - previous)

    gathered = gathered_ref[2]
    for x in (0, top):
        gathered = into_columns(gathered, bars[x], x)
    _, c_end = here.dual_columns(c_dual, c_bar, gathered)
    ends = {x: [dual_end[d, x] for d in range(3)] for x in range(1, 6)}
    for x in (-1, 0, 6, 7):
        ends[x] = here.dual_plane(duals[x], bars[x], bars[x + 1], c_bar, x)
        if x >= 0:
            sums[1] += change_of(ends[x], duals[x]) * (1.0 / STEP_DUAL)
    for x in range(OWN):
        if 2 <= x <= 5:
            u_out[x] = primal_end[x]
        else:
            divergence = ends[x][0] - ends[x - 1][0] + here.across(ends[x], c_end[2], x)
            now = updated(primals[x], plane(4, x), divergence)
            sums[1] += change_of([now], [primals[x]]) * (1.0 / STEP_PRIMAL)
            u_out[x] = now[:ROWS]
        for d in range(3):
            p_out[d, x] = ends[x][d][:ROWS]
    out_lane = lanes_of(8)
    sums_out[...] = jnp.where(
        out_lane == 0, jnp.sum(sums[0]), jnp.where(out_lane == 1, jnp.sum(sums[1]), 0.0)
    )


def shape(*dims):
    return jax.ShapeDtypeStruct(dims, jnp.float32)


def call(kernel, count, outs, scratch=(), specs=None, work=0):
    return pl.pallas_call(
        kernel,
        out_shape=outs,
        in_specs=specs or [VMEM] * count,
        out_specs=jax.tree.map(lambda _: VMEM, outs),
        scratch_shapes=list(scratch),
        compiler_params=pltpu.CompilerParams(vmem_limit_bytes=4 * 2**20),
        cost_estimate=pl.CostEstimate(flops=work, bytes_accessed=work, transcendentals=0),
    )


def trade(first, second, axes):
    count = lax.axis_size(axes)
    outer = [(i, (i + 1 if i % 2 else i - 1) % count) for i in range(count)]
    second = lax.ppermute(second, axes, outer)
    first = lax.ppermute(first, axes, [(i, i ^ 1) for i in range(count)])
    return first, second


def settle(values):
    for axes in (("xl", "core", "xh"), ("z", "y")):
        count = lax.axis_size(axes)
        spread = jnp.broadcast_to(values[:1, :2], (count, 2))
        values = jnp.sum(lax.all_to_all(spread, axes, 0, 0, tiled=True), axis=0, keepdims=True)
    return values[0, :2]


def on_device(f, u, p):
    inputs = [pltpu.with_memory_space_constraint(v, pltpu.HBM) for v in (u, f, p)]
    columns, u, f, p = call(
        load,
        3,
        (shape(ROWS, LANES), shape(*u.shape), shape(*f.shape), shape(*p.shape)),
        [pltpu.SemaphoreType.DMA((3,))],
        [pl.BlockSpec(memory_space=pltpu.HBM)] * 3,
    )(*inputs)
    columns = lax.ppermute(columns, GZ, [(0, 1), (1, 0)])

    message = shape(10, 8, LANES)
    first_y, second_y = trade(*call(y_faces, 4, (message, message))(u, f, p, columns), GY)

    message = shape(5, ALL_ROWS, LANES)
    halo, columns, first, second = call(
        x_faces,
        6,
        (shape(5, OWN, 8, LANES), shape(ALL_ROWS, LANES), message, message),
        [pltpu.VMEM((10, 8, LANES), jnp.float32)] * 2,
    )(u, f, p, columns, second_y, first_y)
    first, second = trade(first, second, GX)

    planes = shape(OWN, ALL_ROWS, LANES)
    triple = shape(3, OWN, ALL_ROWS, LANES)
    done = call(
        early,
        5,
        (
            triple, planes, planes, triple, shape(OWN, ROWS, LANES),
            shape(3, ALL_ROWS, LANES), shape(2, 8, LANES),
        ),
        work=10**6,
    )(u, f, p, halo, columns)
    denoised, dual, sums = call(
        late,
        14,
        (shape(OWN, ROWS, LANES), shape(3, OWN, ROWS, LANES), shape(8, LANES)),
    )(u, f, p, halo, columns, second, first, *done)
    cells = OWN * lax.axis_size(GX) * ROWS * lax.axis_size(GY) * LANES * lax.axis_size(GZ)
    return denoised, dual, jnp.sqrt(settle(sums) / float(cells))


def solution(mesh):
    mesh = Mesh(mesh.devices.reshape(SIZES), ("xl", "z", "core", "y", "xh"))
    placed = (P(GX, GY, GZ), P(GX, GY, GZ), P(None, GX, GY, GZ))
    return jax.shard_map(
        on_device,
        mesh=mesh,
        in_specs=placed,
        out_specs=(P(GX, GY, GZ), P(None, GX, GY, GZ), P()),
        check_vma=False,
    )
```

```python
import jax
import jax.numpy as jnp
from jax import lax
from jax.experimental import pallas as pl
from jax.experimental.pallas import tpu as pltpu
from jax.sharding import Mesh, PartitionSpec as P


GX = ("xl", "z", "core")
GY = "y"
GZ = "xh"
SIZES = (2, 8, 2, 8, 2)

STEP_PRIMAL = 0.25
STEP_DUAL = 0.3
RADIUS = 0.5
OWN = 8
ROWS = 32
ALL_ROWS = 40
LANES = 128
GROUP = 24

VMEM = pl.BlockSpec(memory_space=pltpu.VMEM)


def lanes_of(rows):
    return lax.broadcasted_iota(jnp.int32, (rows, LANES), 1)


def rows_of(rows):
    return lax.broadcasted_iota(jnp.int32, (rows, LANES), 0)


def fields(u_ref, p_ref, f_ref):
    return (u_ref, p_ref.at[0], p_ref.at[1], p_ref.at[2], f_ref)


def next_row(v):
    return pltpu.roll(v, v.shape[0] - 1, 0)


def previous_row(v):
    return pltpu.roll(v, 1, 0)


def turn(v, by):
    return pltpu.roll(v, by % LANES, 1)


def lane_of(x):
    return 2 * (x + 2)


def from_columns(v, x):
    return turn(v, LANES - 1 - lane_of(x))


def into_columns(into, v, x):
    return jnp.where((lanes_of(ALL_ROWS) >> 1) == x + 2, turn(v, lane_of(x) + 1), into)


def load(u_ref, f_ref, p_ref, out_ref, u_vmem, f_vmem, p_vmem, sem):
    sources = fields(u_ref, p_ref, f_ref)
    targets = fields(u_vmem, p_vmem, f_vmem)
    copies = [pltpu.make_async_copy(a, b, sem.at[k]) for k, (a, b) in enumerate(zip(sources, targets))]
    for copy in copies:
        copy.start()
    first = 1 - lax.axis_index(GZ)
    pair = lanes_of(ROWS) >> 1
    columns = jnp.zeros((ROWS, LANES), jnp.float32)
    for g, (copy, field) in enumerate(zip(copies, targets)):
        copy.wait()
        for x in range(OWN):
            lane = g * GROUP + lane_of(x)
            moved = pltpu.roll(field[x], lane + 2 * first, 1)
            columns = jnp.where(pair == lane // 2, moved, columns)
    out_ref[...] = columns


def is_even(axes):
    return lax.rem(lax.axis_index(axes), 2) == 0


def sort_out(even, up, down):
    return jnp.where(even, up, down), jnp.where(even, down, up)


def y_faces(u_ref, f_ref, p_ref, columns_ref, first_ref, second_ref):
    up = [u_ref[:, ROWS - 2, :], u_ref[:, ROWS - 1, :]]
    up += [p_ref[d, :, ROWS - 2, :] for d in range(3)]
    up += [p_ref[d, :, ROWS - 1, :] for d in range(3)]
    up += [f_ref[:, ROWS - 1, :], columns_ref[ROWS - 8 :, :]]
    down = {0: u_ref[:, 0, :], 1: u_ref[:, 1, :], 8: f_ref[:, 0, :], 9: columns_ref[:8, :]}
    down |= {2 + d: p_ref[d, :, 0, :] for d in range(3)}
    even = is_even(GY) == (lax.axis_index("core") == 0)
    for k, tile in enumerate(up):
        first_ref[k], second_ref[k] = sort_out(even, tile, down.get(k, tile))


U_ROWS = ((0, False, 0), (1, False, 1), (6, True, 0), (7, True, 1))
P_ROWS = tuple(((0, False, 2 + d), (6, True, 2 + d), (7, True, 5 + d)) for d in range(3))
F_ROWS = ((0, False, 8), (7, True, 8))
HALO_ROWS = (U_ROWS, *P_ROWS, F_ROWS)


class Local:
    def __init__(self):
        self.size_x = OWN * lax.axis_size(GX)
        size_y = ROWS * lax.axis_size(GY)
        self.start_x = lax.axis_index(GX) * OWN
        start_y = lax.axis_index(GY) * ROWS
        self.later = lax.axis_index(GZ).astype(jnp.float32)
        lane = lanes_of(ALL_ROWS)
        row = rows_of(ALL_ROWS)
        self.lane = lane
        self.odd = (lane & 1) == 1
        self.last_lane = lane == LANES - 1
        self.first_lane = lane == 0
        place_y = start_y + jnp.where(row < ROWS + 4, row, row - ALL_ROWS)
        self.inside_y = jnp.where((place_y >= 0) & (place_y <= size_y - 2), 1.0, 0.0)
        self.inside_z = 1.0 - self.later * jnp.where(self.last_lane, 1.0, 0.0)
        place_x = self.start_x + ((lane % GROUP) >> 1) - 2
        self.inside_h = jnp.where((place_x >= 0) & (place_x <= self.size_x - 2), 1.0, 0.0)
        self.columns_inside = (self.inside_h, self.inside_y, 1.0)

    def inside(self, x):
        place = self.start_x + x
        at_x = jnp.where((place >= 0) & (place <= self.size_x - 2), 1.0, 0.0)
        return (at_x, self.inside_y, self.inside_z)

    def columns_at(self, x):
        return (self.lane >> 1) == x + 2

    def following(self, v, columns, x):
        return jnp.where(self.last_lane, from_columns(columns, x), turn(v, -1))

    def preceding(self, v, columns, x):
        return jnp.where(self.first_lane, self.later * from_columns(columns, x), turn(v, 1))

    def columns_following(self, v, gathered):
        return jnp.where(self.odd, gathered, turn(v, -1))

    def columns_preceding(self, v, gathered):
        return jnp.where(self.odd, turn(v, 1), gathered)

    def move(self, dual, bar, nexts, inside):
        return [p + (STEP_DUAL * i) * (n - bar) for p, n, i in zip(dual, nexts, inside)]

    def project(self, moved, inside):
        square = moved[0] * moved[0] + moved[1] * moved[1] + moved[2] * moved[2]
        scale = RADIUS * lax.rsqrt(jnp.maximum(square, RADIUS * RADIUS))
        return [q * (scale * i) for q, i in zip(moved, inside)]

    def dual_plane(self, dual, bar, above, columns_bar, x):
        nexts = (above, next_row(bar), self.following(bar, columns_bar, x))
        inside = self.inside(x)
        return self.project(self.move(dual, bar, nexts, inside), inside)

    def dual_columns(self, dual, bar, gathered):
        moved = self.move(
            dual,
            bar,
            (turn(bar, -2), next_row(bar), self.columns_following(bar, gathered)),
            self.columns_inside,
        )
        return moved, self.project(moved, self.columns_inside)

    def across(self, dual, columns_z, x):
        return dual[1] - previous_row(dual[1]) + dual[2] - self.preceding(dual[2], columns_z, x)

    def columns_across(self, dual, gathered):
        return (
            dual[1] - previous_row(dual[1]) + dual[2] - self.columns_preceding(dual[2], gathered)
        )


UPDATE = 1.0 / (1.0 + STEP_PRIMAL)
BAR_U = 2.0 * UPDATE - 1.0
BAR_F = 2.0 * UPDATE * STEP_PRIMAL


def updated(u, f, divergence):
    return (u + STEP_PRIMAL * (divergence + f)) * UPDATE


def early_bar(u, f):
    return BAR_U * u + BAR_F * f


def fold(v):
    return v[0:8] + v[8:16] + v[16:24] + v[24:32]


def change_of(new, old):
    return sum(fold((n - o) * (n - o)) for n, o in zip(new, old))


def plane_of(u_ref, f_ref, p_ref, halo_ref):
    sources = fields(u_ref, p_ref, f_ref)

    def plane(field, x):
        return jnp.concatenate([sources[field][x], halo_ref[field, x]], axis=0)

    def dual(x):
        return [plane(1 + d, x) for d in range(3)]

    return plane, dual


def split(columns):
    u, p0, p1, p2, f = [turn(columns, -GROUP * g) for g in range(5)]
    return u, [p0, p1, p2], f


def zeros():
    return jnp.zeros((ALL_ROWS, LANES), jnp.float32)


def gather(v, planes):
    into = zeros()
    for x in planes:
        into = into_columns(into, v(x), x)
    return into


def x_faces(
    u_ref, f_ref, p_ref, columns_ref, second_y_ref, first_y_ref,
    halo_ref, columns_out, first_ref, second_ref, below_s, above_s,
):
    even = is_even(GY) == (lax.axis_index("core") == 0)
    for k in range(10):
        above_s[k], below_s[k] = sort_out(even, first_y_ref[k], second_y_ref[k])
    for field in range(5):
        for x in range(OWN):
            halo_ref[field, x] = jnp.zeros((8, LANES), jnp.float32)
            for row, from_below, tile in HALO_ROWS[field]:
                source = below_s if from_below else above_s
                halo_ref[field, x, row : row + 1, :] = source[tile, x : x + 1, :]
    row = rows_of(8)
    columns_out[:ROWS, :] = columns_ref[...]
    columns_out[ROWS:, :] = jnp.where(row >= 6, below_s[9], jnp.where(row < 2, above_s[9], 0.0))

    here = Local()
    plane, dual = plane_of(u_ref, f_ref, p_ref, halo_ref)
    c_u, c_p, c_f = split(columns_out[...])
    c_moved, c_dual = here.dual_columns(c_p, c_u, gather(lambda x: plane(0, x), range(OWN)))

    top = OWN - 1
    u, p = plane(0, top), dual(top)
    nexts = (0.0, next_row(u), here.following(u, c_u, top))
    moved = here.move(p, u, nexts, (1.0, here.inside_y, here.inside_z))
    last = here.dual_plane(dual(top - 1), plane(0, top - 1), u, c_u, top - 1)
    up = [*moved, early_bar(u, plane(4, top)) - BAR_F * last[0]]
    c_up = [
        c_p[0] - STEP_DUAL * c_u, c_moved[1], c_moved[2],
        early_bar(c_u, c_f) - BAR_F * turn(c_dual[0], 2),
    ]

    u = plane(0, 0)
    new = here.dual_plane(dual(0), u, plane(0, 1), c_u, 0)
    bar = early_bar(u, plane(4, 0)) + BAR_F * (new[0] + here.across(new, c_dual[2], 0))
    down = [u, bar]
    gathered = into_columns(zeros(), new[2], 0)
    c_bar = early_bar(c_u, c_f) + BAR_F * (c_dual[0] + here.columns_across(c_dual, gathered))
    c_down = [c_u, c_bar]

    def packed(parts):
        group = here.lane // GROUP
        whole = parts[0]
        for k, part in enumerate(parts[1:], 1):
            whole = jnp.where(group == k, turn(part, GROUP * k), whole)
        return whole

    up.append(packed(c_up))
    down = [*down, up[2], up[3], packed(c_down)]
    even = is_even(GX)
    for k in range(5):
        first_ref[k], second_ref[k] = sort_out(even, up[k], down[k])


def early(
    u_ref, f_ref, p_ref, halo_ref, columns_ref,
    dual_out, bar_out, primal_out, dual_end, primal_end, gathered_out, sums_out,
):
    here = Local()
    plane, dual = plane_of(u_ref, f_ref, p_ref, halo_ref)
    c_u, c_p, c_f = split(columns_ref[...])
    sums = [jnp.zeros((8, LANES), jnp.float32) for _ in range(2)]

    gathered_u = gather(lambda x: plane(0, x), range(OWN))
    _, c_dual = here.dual_columns(c_p, c_u, gathered_u)
    gathered_dual = zeros()
    gathered_bar = zeros()
    for x in range(7):
        old = dual(x)
        u = plane(0, x)
        new = here.dual_plane(old, u, plane(0, x + 1), c_u, x)
        sums[0] += change_of(new, old) * (1.0 / STEP_DUAL)
        gathered_dual = into_columns(gathered_dual, new[2], x)
        for d in range(3):
            dual_out[d, x] = new[d]
        if x > 0:
            divergence = new[0] - previous + here.across(new, c_dual[2], x)
            now = updated(u, plane(4, x), divergence)
            bar = 2.0 * now - u
            sums[0] += change_of([now], [u]) * (1.0 / STEP_PRIMAL)
            gathered_bar = into_columns(gathered_bar, bar, x)
            primal_out[x] = now
            bar_out[x] = bar
        previous = new[0]
    divergence = c_dual[0] - turn(c_dual[0], 2) + here.columns_across(c_dual, gathered_dual)
    c_bar = early_bar(c_u, c_f) + BAR_F * divergence

    _, c_end = here.dual_columns(c_dual, c_bar, gathered_bar)
    for x in range(1, 6):
        old = [dual_out[d, x] for d in range(3)]
        new = here.dual_plane(old, bar_out[x], bar_out[x + 1], c_bar, x)
        sums[1] += change_of(new, old) * (1.0 / STEP_DUAL)
        for d in range(3):
            dual_end[d, x] = new[d]
        if x > 1:
            u = primal_out[x]
            divergence = new[0] - previous + here.across(new, c_end[2], x)
            now = updated(u, plane(4, x), divergence)
            sums[1] += change_of([now], [u]) * (1.0 / STEP_PRIMAL)
            primal_end[x] = now[:ROWS]
        previous = new[0]
    for k, v in enumerate((gathered_u, gathered_dual, gathered_bar)):
        gathered_out[k] = v
    for k in range(2):
        sums_out[k] = sums[k]


def late(
    u_ref, f_ref, p_ref, halo_ref, columns_ref, second_x_ref, first_x_ref,
    dual_ref, bar_ref, primal_ref, dual_end, primal_end, gathered_ref, early_sums,
    u_out, p_out, sums_out,
):
    here = Local()
    plane, dual = plane_of(u_ref, f_ref, p_ref, halo_ref)
    even = is_even(GX)
    above, below = zip(*[sort_out(even, first_x_ref[k], second_x_ref[k]) for k in range(5)])
    sums = [early_sums[0], early_sums[1]]

    c_u, c_p, c_f = split(columns_ref[...])
    lowest, highest = here.columns_at(-1), here.columns_at(OWN)

    def from_below(k):
        return turn(below[4], -GROUP * k - 16)

    def from_above(k):
        return turn(above[4], -GROUP * k + 16)

    c_u = jnp.where(highest, from_above(0), c_u)
    c_moved, _ = here.dual_columns(c_p, c_u, gathered_ref[0])
    sent = (from_below(0) + STEP_DUAL * turn(c_u, -2), from_below(1), from_below(2))
    c_moved = [jnp.where(lowest, s, m) for s, m in zip(sent, c_moved)]
    c_dual = here.project(c_moved, here.columns_inside)

    duals = {x: [dual_ref[d, x] for d in range(3)] for x in range(7)}
    bars = {x: bar_ref[x] for x in range(1, 7)}
    primals = {x: primal_ref[x] for x in range(1, 7)}
    top = OWN - 1
    moved = (below[0] + STEP_DUAL * plane(0, 0), below[1], below[2])
    duals[-1] = here.project(moved, here.inside(-1))
    old = dual(top)
    duals[top] = here.dual_plane(old, plane(0, top), above[0], c_u, top)
    sums[0] += change_of(duals[top], old) * (1.0 / STEP_DUAL)
    for x in (0, top):
        u = plane(0, x)
        divergence = duals[x][0] - duals[x - 1][0] + here.across(duals[x], c_dual[2], x)
        primals[x] = updated(u, plane(4, x), divergence)
        bars[x] = 2.0 * primals[x] - u
        sums[0] += change_of([primals[x]], [u]) * (1.0 / STEP_PRIMAL)
    bars[-1] = below[3] + BAR_F * (duals[-1][0] + here.across(duals[-1], c_dual[2], -1))
    bars[OWN] = above[1] - BAR_F * duals[top][0]

    gathered = gathered_ref[1]
    for x in (-1, top):
        gathered = into_columns(gathered, duals[x][2], x)
    known = jnp.where(
        lowest, from_below(3), jnp.where(highest, from_above(1), early_bar(c_u, c_f))
    )
    own_part = jnp.where(highest, 0.0, c_dual[0] + here.columns_across(c_dual, gathered))
    previous = jnp.where(lowest, 0.0, turn(c_dual[0], 2))
    c_bar = known + BAR_F * (own_part - previous)

    gathered = gathered_ref[2]
    for x in (0, top):
        gathered = into_columns(gathered, bars[x], x)
    _, c_end = here.dual_columns(c_dual, c_bar, gathered)
    ends = {x: [dual_end[d, x] for d in range(3)] for x in range(1, 6)}
    for x in (-1, 0, 6, 7):
        ends[x] = here.dual_plane(duals[x], bars[x], bars[x + 1], c_bar, x)
        if x >= 0:
            sums[1] += change_of(ends[x], duals[x]) * (1.0 / STEP_DUAL)
    for x in range(OWN):
        if 2 <= x <= 5:
            u_out[x] = primal_end[x]
        else:
            divergence = ends[x][0] - ends[x - 1][0] + here.across(ends[x], c_end[2], x)
            now = updated(primals[x], plane(4, x), divergence)
            sums[1] += change_of([now], [primals[x]]) * (1.0 / STEP_PRIMAL)
            u_out[x] = now[:ROWS]
        for d in range(3):
            p_out[d, x] = ends[x][d][:ROWS]
    out_lane = lanes_of(8)
    sums_out[...] = jnp.where(
        out_lane == 0, jnp.sum(sums[0]), jnp.where(out_lane == 1, jnp.sum(sums[1]), 0.0)
    )


def shape(*dims):
    return jax.ShapeDtypeStruct(dims, jnp.float32)


def call(kernel, count, outs, scratch=(), specs=None, work=0):
    return pl.pallas_call(
        kernel,
        out_shape=outs,
        in_specs=specs or [VMEM] * count,
        out_specs=jax.tree.map(lambda _: VMEM, outs),
        scratch_shapes=list(scratch),
        compiler_params=pltpu.CompilerParams(vmem_limit_bytes=4 * 2**20),
        cost_estimate=pl.CostEstimate(flops=work, bytes_accessed=work, transcendentals=0),
    )


def trade_y(first, second):
    count = lax.axis_size(GY)
    inner = [i ^ 1 for i in range(count)]
    outer = [(i + 1 if i % 2 else i - 1) % count for i in range(count)]

    def pairs(on_first, on_second):
        return [(i, j) for i, j in enumerate(on_first)] + [
            (count + i, count + j) for i, j in enumerate(on_second)
        ]

    second = lax.ppermute(second, ("core", GY), pairs(outer, inner))
    first = lax.ppermute(first, ("core", GY), pairs(inner, outer))
    return first, second


def trade(first, second, axes):
    count = lax.axis_size(axes)
    outer = [(i, (i + 1 if i % 2 else i - 1) % count) for i in range(count)]
    second = lax.ppermute(second, axes, outer)
    first = lax.ppermute(first, axes, [(i, i ^ 1) for i in range(count)])
    return first, second


STAGES = ((("xl", "core", "y", "xh"), ((0 * 2 + 1) * 8 + 4) * 2 + 1), (("z",), 5))


def settle(rows):
    values = rows[:1, :2]
    for axes, member in STAGES:
        count = lax.axis_size(axes)
        order = [member] + [i for i in range(count) if i != member]
        spread = jnp.broadcast_to(values, (count, 2))
        spread = lax.all_to_all(spread, axes, 0, 0, tiled=True, axis_index_groups=[order])
        values = jnp.sum(spread, axis=0, keepdims=True)
    return values[0, :2]


def on_device(f, u, p):
    inputs = [pltpu.with_memory_space_constraint(v, pltpu.HBM) for v in (u, f, p)]
    columns, u, f, p = call(
        load,
        3,
        (shape(ROWS, LANES), shape(*u.shape), shape(*f.shape), shape(*p.shape)),
        [pltpu.SemaphoreType.DMA((5,))],
        [pl.BlockSpec(memory_space=pltpu.HBM)] * 3,
    )(*inputs)
    columns = lax.ppermute(columns, GZ, [(0, 1), (1, 0)])

    message = shape(10, 8, LANES)
    first_y, second_y = trade_y(*call(y_faces, 4, (message, message))(u, f, p, columns))

    message = shape(5, ALL_ROWS, LANES)
    halo, columns, first, second = call(
        x_faces,
        6,
        (shape(5, OWN, 8, LANES), shape(ALL_ROWS, LANES), message, message),
        [pltpu.VMEM((10, 8, LANES), jnp.float32)] * 2,
    )(u, f, p, columns, second_y, first_y)
    first, second = trade(first, second, GX)

    planes = shape(OWN, ALL_ROWS, LANES)
    triple = shape(3, OWN, ALL_ROWS, LANES)
    done = call(
        early,
        5,
        (
            triple, planes, planes, triple, shape(OWN, ROWS, LANES),
            shape(3, ALL_ROWS, LANES), shape(2, 8, LANES),
        ),
        work=10**6,
    )(u, f, p, halo, columns)
    denoised, dual, sums = call(
        late,
        14,
        (shape(OWN, ROWS, LANES), shape(3, OWN, ROWS, LANES), shape(8, LANES)),
    )(u, f, p, halo, columns, second, first, *done)
    cells = OWN * lax.axis_size(GX) * ROWS * lax.axis_size(GY) * LANES * lax.axis_size(GZ)
    return denoised, dual, jnp.sqrt(settle(sums) / float(cells))


def solution(mesh):
    mesh = Mesh(mesh.devices.reshape(SIZES), ("xl", "z", "core", "y", "xh"))
    placed = (P(GX, GY, GZ), P(GX, GY, GZ), P(None, GX, GY, GZ))
    return jax.shard_map(
        on_device,
        mesh=mesh,
        in_specs=placed,
        out_specs=(P(GX, GY, GZ), P(None, GX, GY, GZ), P()),
        check_vma=False,
    )
```

```python
import jax
import jax.numpy as jnp
from jax import lax
from jax.experimental import pallas as pl
from jax.experimental.pallas import tpu as pltpu
from jax.sharding import Mesh, PartitionSpec as P


GX = ("xl", "z", "core")
GY = "y"
GZ = "xh"
SIZES = (2, 8, 2, 8, 2)

STEP_PRIMAL = 0.25
STEP_DUAL = 0.3
RADIUS = 0.5
OWN = 8
ROWS = 32
ALL_ROWS = 40
LANES = 128
GROUP = 24

VMEM = pl.BlockSpec(memory_space=pltpu.VMEM)


def lanes_of(rows):
    return lax.broadcasted_iota(jnp.int32, (rows, LANES), 1)


def rows_of(rows):
    return lax.broadcasted_iota(jnp.int32, (rows, LANES), 0)


def fields(u_ref, p_ref, f_ref):
    return (u_ref, p_ref.at[0], p_ref.at[1], p_ref.at[2], f_ref)


def next_row(v):
    return pltpu.roll(v, v.shape[0] - 1, 0)


def previous_row(v):
    return pltpu.roll(v, 1, 0)


def turn(v, by):
    return pltpu.roll(v, by % LANES, 1)


def lane_of(x):
    return 2 * (x + 2)


def from_columns(v, x):
    return turn(v, LANES - 1 - lane_of(x))


def into_columns(into, v, x):
    return jnp.where((lanes_of(ALL_ROWS) >> 1) == x + 2, turn(v, lane_of(x) + 1), into)


def load(u_ref, f_ref, p_ref, out_ref, u_vmem, f_vmem, p_vmem, sem):
    arrays = ((u_ref, u_vmem), (p_ref, p_vmem), (f_ref, f_vmem))
    copies = [pltpu.make_async_copy(a, b, sem.at[k]) for k, (a, b) in enumerate(arrays)]
    for copy in copies:
        copy.start()
    first = 1 - lax.axis_index(GZ)
    pair = lanes_of(ROWS) >> 1
    columns = jnp.zeros((ROWS, LANES), jnp.float32)
    for g, field in enumerate(fields(u_vmem, p_vmem, f_vmem)):
        if g in (0, 1, 4):
            copies[(g + 1) // 2].wait()
        for x in range(OWN):
            lane = g * GROUP + lane_of(x)
            moved = pltpu.roll(field[x], lane + 2 * first, 1)
            columns = jnp.where(pair == lane // 2, moved, columns)
    out_ref[...] = columns


def is_even(axes):
    return lax.rem(lax.axis_index(axes), 2) == 0


def sort_out(even, up, down):
    return jnp.where(even, up, down), jnp.where(even, down, up)


def y_faces(u_ref, f_ref, p_ref, columns_ref, first_ref, second_ref):
    up = [u_ref[:, ROWS - 2, :], u_ref[:, ROWS - 1, :]]
    up += [p_ref[d, :, ROWS - 2, :] for d in range(3)]
    up += [p_ref[d, :, ROWS - 1, :] for d in range(3)]
    up += [f_ref[:, ROWS - 1, :], columns_ref[ROWS - 8 :, :]]
    down = {0: u_ref[:, 0, :], 1: u_ref[:, 1, :], 8: f_ref[:, 0, :], 9: columns_ref[:8, :]}
    down |= {2 + d: p_ref[d, :, 0, :] for d in range(3)}
    even = is_even(GY)
    for k, tile in enumerate(up):
        first_ref[k], second_ref[k] = sort_out(even, tile, down.get(k, tile))


U_ROWS = ((0, False, 0), (1, False, 1), (6, True, 0), (7, True, 1))
P_ROWS = tuple(((0, False, 2 + d), (6, True, 2 + d), (7, True, 5 + d)) for d in range(3))
F_ROWS = ((0, False, 8), (7, True, 8))
HALO_ROWS = (U_ROWS, *P_ROWS, F_ROWS)


class Local:
    def __init__(self):
        self.size_x = OWN * lax.axis_size(GX)
        size_y = ROWS * lax.axis_size(GY)
        self.start_x = lax.axis_index(GX) * OWN
        start_y = lax.axis_index(GY) * ROWS
        self.later = lax.axis_index(GZ).astype(jnp.float32)
        lane = lanes_of(ALL_ROWS)
        row = rows_of(ALL_ROWS)
        self.lane = lane
        self.odd = (lane & 1) == 1
        self.last_lane = lane == LANES - 1
        self.first_lane = lane == 0
        place_y = start_y + jnp.where(row < ROWS + 4, row, row - ALL_ROWS)
        self.inside_y = jnp.where((place_y >= 0) & (place_y <= size_y - 2), 1.0, 0.0)
        self.inside_z = 1.0 - self.later * jnp.where(self.last_lane, 1.0, 0.0)
        place_x = self.start_x + ((lane % GROUP) >> 1) - 2
        self.inside_h = jnp.where((place_x >= 0) & (place_x <= self.size_x - 2), 1.0, 0.0)
        self.columns_inside = (self.inside_h, self.inside_y, 1.0)

    def inside(self, x):
        place = self.start_x + x
        at_x = jnp.where((place >= 0) & (place <= self.size_x - 2), 1.0, 0.0)
        return (at_x, self.inside_y, self.inside_z)

    def columns_at(self, x):
        return (self.lane >> 1) == x + 2

    def following(self, v, columns, x):
        return jnp.where(self.last_lane, from_columns(columns, x), turn(v, -1))

    def preceding(self, v, columns, x):
        return jnp.where(self.first_lane, self.later * from_columns(columns, x), turn(v, 1))

    def columns_following(self, v, gathered):
        return jnp.where(self.odd, gathered, turn(v, -1))

    def columns_preceding(self, v, gathered):
        return jnp.where(self.odd, turn(v, 1), gathered)

    def move(self, dual, bar, nexts, inside):
        return [p + (STEP_DUAL * i) * (n - bar) for p, n, i in zip(dual, nexts, inside)]

    def project(self, moved, inside):
        square = moved[0] * moved[0] + moved[1] * moved[1] + moved[2] * moved[2]
        scale = RADIUS * lax.rsqrt(jnp.maximum(square, RADIUS * RADIUS))
        return [q * (scale * i) for q, i in zip(moved, inside)]

    def dual_plane(self, dual, bar, above, columns_bar, x):
        nexts = (above, next_row(bar), self.following(bar, columns_bar, x))
        inside = self.inside(x)
        return self.project(self.move(dual, bar, nexts, inside), inside)

    def dual_columns(self, dual, bar, gathered):
        moved = self.move(
            dual,
            bar,
            (turn(bar, -2), next_row(bar), self.columns_following(bar, gathered)),
            self.columns_inside,
        )
        return moved, self.project(moved, self.columns_inside)

    def across(self, dual, columns_z, x):
        return dual[1] - previous_row(dual[1]) + dual[2] - self.preceding(dual[2], columns_z, x)

    def columns_across(self, dual, gathered):
        return (
            dual[1] - previous_row(dual[1]) + dual[2] - self.columns_preceding(dual[2], gathered)
        )


UPDATE = 1.0 / (1.0 + STEP_PRIMAL)
BAR_U = 2.0 * UPDATE - 1.0
BAR_F = 2.0 * UPDATE * STEP_PRIMAL


def updated(u, f, divergence):
    return (u + STEP_PRIMAL * (divergence + f)) * UPDATE


def early_bar(u, f):
    return BAR_U * u + BAR_F * f


def fold(v):
    return v[0:8] + v[8:16] + v[16:24] + v[24:32]


def change_of(new, old):
    return sum(fold((n - o) * (n - o)) for n, o in zip(new, old))


def plane_of(u_ref, f_ref, p_ref, halo_ref):
    sources = fields(u_ref, p_ref, f_ref)

    def plane(field, x):
        return jnp.concatenate([sources[field][x], halo_ref[field, x]], axis=0)

    def dual(x):
        return [plane(1 + d, x) for d in range(3)]

    return plane, dual


def split(columns):
    u, p0, p1, p2, f = [turn(columns, -GROUP * g) for g in range(5)]
    return u, [p0, p1, p2], f


def zeros():
    return jnp.zeros((ALL_ROWS, LANES), jnp.float32)


def gather(v, planes):
    into = zeros()
    for x in planes:
        into = into_columns(into, v(x), x)
    return into


def x_faces(
    u_ref, f_ref, p_ref, columns_ref, second_y_ref, first_y_ref,
    halo_ref, columns_out, first_ref, second_ref, below_s, above_s,
):
    even = is_even(GY)
    for k in range(10):
        above_s[k], below_s[k] = sort_out(even, first_y_ref[k], second_y_ref[k])
    for field in range(5):
        for x in range(OWN):
            halo_ref[field, x] = jnp.zeros((8, LANES), jnp.float32)
            for row, from_below, tile in HALO_ROWS[field]:
                source = below_s if from_below else above_s
                halo_ref[field, x, row : row + 1, :] = source[tile, x : x + 1, :]
    row = rows_of(8)
    columns_out[:ROWS, :] = columns_ref[...]
    columns_out[ROWS:, :] = jnp.where(row >= 6, below_s[9], jnp.where(row < 2, above_s[9], 0.0))

    here = Local()
    plane, dual = plane_of(u_ref, f_ref, p_ref, halo_ref)
    c_u, c_p, c_f = split(columns_out[...])
    c_moved, c_dual = here.dual_columns(c_p, c_u, gather(lambda x: plane(0, x), (0, 6, 7)))

    top = OWN - 1
    u, p = plane(0, top), dual(top)
    nexts = (0.0, next_row(u), here.following(u, c_u, top))
    moved = here.move(p, u, nexts, (1.0, here.inside_y, here.inside_z))
    last = here.dual_plane(dual(top - 1), plane(0, top - 1), u, c_u, top - 1)
    up = [*moved, early_bar(u, plane(4, top)) - BAR_F * last[0]]
    c_up = [
        c_p[0] - STEP_DUAL * c_u, c_moved[1], c_moved[2],
        early_bar(c_u, c_f) - BAR_F * turn(c_dual[0], 2),
    ]

    u = plane(0, 0)
    new = here.dual_plane(dual(0), u, plane(0, 1), c_u, 0)
    bar = early_bar(u, plane(4, 0)) + BAR_F * (new[0] + here.across(new, c_dual[2], 0))
    down = [u, bar]
    gathered = into_columns(zeros(), new[2], 0)
    c_bar = early_bar(c_u, c_f) + BAR_F * (c_dual[0] + here.columns_across(c_dual, gathered))
    c_down = [c_u, c_bar]

    def packed(parts):
        group = here.lane // GROUP
        whole = parts[0]
        for k, part in enumerate(parts[1:], 1):
            whole = jnp.where(group == k, turn(part, GROUP * k), whole)
        return whole

    up.append(packed(c_up))
    down = [*down, up[2], up[3], packed(c_down)]
    even = is_even(GX)
    for k in range(5):
        first_ref[k], second_ref[k] = sort_out(even, up[k], down[k])


def early(
    u_ref, f_ref, p_ref, halo_ref, columns_ref,
    dual_out, bar_out, primal_out, dual_end, primal_end, gathered_out, sums_out,
):
    here = Local()
    plane, dual = plane_of(u_ref, f_ref, p_ref, halo_ref)
    c_u, c_p, c_f = split(columns_ref[...])
    sums = [jnp.zeros((8, LANES), jnp.float32) for _ in range(2)]

    gathered_u = gather(lambda x: plane(0, x), range(OWN))
    _, c_dual = here.dual_columns(c_p, c_u, gathered_u)
    gathered_dual = zeros()
    gathered_bar = zeros()
    for x in range(7):
        old = dual(x)
        u = plane(0, x)
        new = here.dual_plane(old, u, plane(0, x + 1), c_u, x)
        sums[0] += change_of(new, old) * (1.0 / STEP_DUAL)
        gathered_dual = into_columns(gathered_dual, new[2], x)
        for d in range(3):
            dual_out[d, x] = new[d]
        if x > 0:
            divergence = new[0] - previous + here.across(new, c_dual[2], x)
            now = updated(u, plane(4, x), divergence)
            bar = 2.0 * now - u
            sums[0] += change_of([now], [u]) * (1.0 / STEP_PRIMAL)
            gathered_bar = into_columns(gathered_bar, bar, x)
            primal_out[x] = now
            bar_out[x] = bar
        previous = new[0]
    divergence = c_dual[0] - turn(c_dual[0], 2) + here.columns_across(c_dual, gathered_dual)
    c_bar = early_bar(c_u, c_f) + BAR_F * divergence

    _, c_end = here.dual_columns(c_dual, c_bar, gathered_bar)
    for x in range(1, 6):
        old = [dual_out[d, x] for d in range(3)]
        new = here.dual_plane(old, bar_out[x], bar_out[x + 1], c_bar, x)
        sums[1] += change_of(new, old) * (1.0 / STEP_DUAL)
        for d in range(3):
            dual_end[d, x] = new[d]
        if x > 1:
            u = primal_out[x]
            divergence = new[0] - previous + here.across(new, c_end[2], x)
            now = updated(u, plane(4, x), divergence)
            sums[1] += change_of([now], [u]) * (1.0 / STEP_PRIMAL)
            primal_end[x] = now[:ROWS]
        previous = new[0]
    for k, v in enumerate((gathered_u, gathered_dual, gathered_bar)):
        gathered_out[k] = v
    for k in range(2):
        sums_out[k] = sums[k]


def late(
    u_ref, f_ref, p_ref, halo_ref, columns_ref, second_x_ref, first_x_ref,
    dual_ref, bar_ref, primal_ref, dual_end, primal_end, gathered_ref, early_sums,
    u_out, p_out, sums_out,
):
    here = Local()
    plane, dual = plane_of(u_ref, f_ref, p_ref, halo_ref)
    even = is_even(GX)
    above, below = zip(*[sort_out(even, first_x_ref[k], second_x_ref[k]) for k in range(5)])
    sums = [early_sums[0], early_sums[1]]

    c_u, c_p, c_f = split(columns_ref[...])
    lowest, highest = here.columns_at(-1), here.columns_at(OWN)

    def from_below(k):
        return turn(below[4], -GROUP * k - 16)

    def from_above(k):
        return turn(above[4], -GROUP * k + 16)

    c_u = jnp.where(highest, from_above(0), c_u)
    c_moved, _ = here.dual_columns(c_p, c_u, gathered_ref[0])
    sent = (from_below(0) + STEP_DUAL * turn(c_u, -2), from_below(1), from_below(2))
    c_moved = [jnp.where(lowest, s, m) for s, m in zip(sent, c_moved)]
    c_dual = here.project(c_moved, here.columns_inside)

    duals = {x: [dual_ref[d, x] for d in range(3)] for x in range(7)}
    bars = {x: bar_ref[x] for x in range(1, 7)}
    primals = {x: primal_ref[x] for x in range(1, 7)}
    top = OWN - 1
    moved = (below[0] + STEP_DUAL * plane(0, 0), below[1], below[2])
    duals[-1] = here.project(moved, here.inside(-1))
    old = dual(top)
    duals[top] = here.dual_plane(old, plane(0, top), above[0], c_u, top)
    sums[0] += change_of(duals[top], old) * (1.0 / STEP_DUAL)
    for x in (0, top):
        u = plane(0, x)
        divergence = duals[x][0] - duals[x - 1][0] + here.across(duals[x], c_dual[2], x)
        primals[x] = updated(u, plane(4, x), divergence)
        bars[x] = 2.0 * primals[x] - u
        sums[0] += change_of([primals[x]], [u]) * (1.0 / STEP_PRIMAL)
    bars[-1] = below[3] + BAR_F * (duals[-1][0] + here.across(duals[-1], c_dual[2], -1))
    bars[OWN] = above[1] - BAR_F * duals[top][0]

    gathered = gathered_ref[1]
    for x in (-1, top):
        gathered = into_columns(gathered, duals[x][2], x)
    known = jnp.where(
        lowest, from_below(3), jnp.where(highest, from_above(1), early_bar(c_u, c_f))
    )
    own_part = jnp.where(highest, 0.0, c_dual[0] + here.columns_across(c_dual, gathered))
    previous = jnp.where(lowest, 0.0, turn(c_dual[0], 2))
    c_bar = known + BAR_F * (own_part - previous)

    gathered = gathered_ref[2]
    for x in (0, top):
        gathered = into_columns(gathered, bars[x], x)
    _, c_end = here.dual_columns(c_dual, c_bar, gathered)
    ends = {x: [dual_end[d, x] for d in range(3)] for x in range(1, 6)}
    for x in (-1, 0, 6, 7):
        ends[x] = here.dual_plane(duals[x], bars[x], bars[x + 1], c_bar, x)
        if x >= 0:
            sums[1] += change_of(ends[x], duals[x]) * (1.0 / STEP_DUAL)
    for x in range(OWN):
        if 2 <= x <= 5:
            u_out[x] = primal_end[x]
        else:
            divergence = ends[x][0] - ends[x - 1][0] + here.across(ends[x], c_end[2], x)
            now = updated(primals[x], plane(4, x), divergence)
            sums[1] += change_of([now], [primals[x]]) * (1.0 / STEP_PRIMAL)
            u_out[x] = now[:ROWS]
        for d in range(3):
            p_out[d, x] = ends[x][d][:ROWS]
    out_lane = lanes_of(8)
    sums_out[...] = jnp.where(
        out_lane == 0, jnp.sum(sums[0]), jnp.where(out_lane == 1, jnp.sum(sums[1]), 0.0)
    )


def shape(*dims):
    return jax.ShapeDtypeStruct(dims, jnp.float32)


def call(kernel, count, outs, scratch=(), specs=None, work=0):
    return pl.pallas_call(
        kernel,
        out_shape=outs,
        in_specs=specs or [VMEM] * count,
        out_specs=jax.tree.map(lambda _: VMEM, outs),
        scratch_shapes=list(scratch),
        compiler_params=pltpu.CompilerParams(vmem_limit_bytes=4 * 2**20),
        cost_estimate=pl.CostEstimate(flops=work, bytes_accessed=work, transcendentals=0),
    )


def trade(first, second, axes):
    count = lax.axis_size(axes)
    outer = [(i, (i + 1 if i % 2 else i - 1) % count) for i in range(count)]
    second = lax.ppermute(second, axes, outer)
    first = lax.ppermute(first, axes, [(i, i ^ 1) for i in range(count)])
    return first, second


STAGES = ((("core", "y"), 12), (("xl", "z", "xh"), (0 * 8 + 5) * 2 + 1))


def settle(rows):
    values = rows[:1, :2]
    for axes, member in STAGES:
        count = lax.axis_size(axes)
        order = [member] + [i for i in range(count) if i != member]
        spread = jnp.broadcast_to(values, (count, 2))
        spread = lax.all_to_all(spread, axes, 0, 0, tiled=True, axis_index_groups=[order])
        values = jnp.sum(spread, axis=0, keepdims=True)
    return values[0, :2]


def on_device(f, u, p):
    inputs = [pltpu.with_memory_space_constraint(v, pltpu.HBM) for v in (u, f, p)]
    columns, u, f, p = call(
        load,
        3,
        (shape(ROWS, LANES), shape(*u.shape), shape(*f.shape), shape(*p.shape)),
        [pltpu.SemaphoreType.DMA((3,))],
        [pl.BlockSpec(memory_space=pltpu.HBM)] * 3,
    )(*inputs)
    columns = lax.ppermute(columns, GZ, [(0, 1), (1, 0)])

    message = shape(10, 8, LANES)
    first_y, second_y = trade(*call(y_faces, 4, (message, message))(u, f, p, columns), GY)

    message = shape(5, ALL_ROWS, LANES)
    halo, columns, first, second = call(
        x_faces,
        6,
        (shape(5, OWN, 8, LANES), shape(ALL_ROWS, LANES), message, message),
        [pltpu.VMEM((10, 8, LANES), jnp.float32)] * 2,
    )(u, f, p, columns, second_y, first_y)
    first, second = trade(first, second, GX)

    planes = shape(OWN, ALL_ROWS, LANES)
    triple = shape(3, OWN, ALL_ROWS, LANES)
    done = call(
        early,
        5,
        (
            triple, planes, planes, triple, shape(OWN, ROWS, LANES),
            shape(3, ALL_ROWS, LANES), shape(2, 8, LANES),
        ),
        work=10**6,
    )(u, f, p, halo, columns)
    denoised, dual, sums = call(
        late,
        14,
        (shape(OWN, ROWS, LANES), shape(3, OWN, ROWS, LANES), shape(8, LANES)),
    )(u, f, p, halo, columns, second, first, *done)
    cells = OWN * lax.axis_size(GX) * ROWS * lax.axis_size(GY) * LANES * lax.axis_size(GZ)
    return denoised, dual, jnp.sqrt(settle(sums) / float(cells))


def solution(mesh):
    mesh = Mesh(mesh.devices.reshape(SIZES), ("xl", "z", "core", "y", "xh"))
    placed = (P(GX, GY, GZ), P(GX, GY, GZ), P(None, GX, GY, GZ))
    return jax.shard_map(
        on_device,
        mesh=mesh,
        in_specs=placed,
        out_specs=(P(GX, GY, GZ), P(None, GX, GY, GZ), P()),
        check_vma=False,
    )
```

```python
import jax
import jax.numpy as jnp
from jax import lax
from jax.experimental import pallas as pl
from jax.experimental.pallas import tpu as pltpu
from jax.sharding import Mesh, PartitionSpec as P


GX = ("xl", "z", "core")
GY = "y"
GZ = "xh"
SIZES = (2, 8, 2, 8, 2)

STEP_PRIMAL = 0.25
STEP_DUAL = 0.3
RADIUS = 0.5
OWN = 8
ROWS = 32
ALL_ROWS = 40
LANES = 128
GROUP = 24

VMEM = pl.BlockSpec(memory_space=pltpu.VMEM)
HBM = pl.BlockSpec(memory_space=pltpu.HBM)


def lanes_of(rows):
    return lax.broadcasted_iota(jnp.int32, (rows, LANES), 1)


def rows_of(rows):
    return lax.broadcasted_iota(jnp.int32, (rows, LANES), 0)


def fields(u_ref, p_ref, f_ref):
    return (u_ref, p_ref.at[0], p_ref.at[1], p_ref.at[2], f_ref)


def next_row(v):
    return pltpu.roll(v, v.shape[0] - 1, 0)


def previous_row(v):
    return pltpu.roll(v, 1, 0)


def turn(v, by):
    return pltpu.roll(v, by % LANES, 1)


def lane_of(x):
    return 2 * (x + 2)


def from_columns(v, x):
    return turn(v, LANES - 1 - lane_of(x))


def into_columns(into, v, x):
    return jnp.where((lanes_of(ALL_ROWS) >> 1) == x + 2, turn(v, lane_of(x) + 1), into)


def load(u_ref, f_ref, p_ref, out_ref, u_vmem, f_vmem, p_vmem, sem):
    arrays = ((u_ref, u_vmem), (p_ref, p_vmem), (f_ref, f_vmem))
    copies = [pltpu.make_async_copy(a, b, sem.at[k]) for k, (a, b) in enumerate(arrays)]
    for copy in copies:
        copy.start()
    first = 1 - lax.axis_index(GZ)
    pair = lanes_of(ROWS) >> 1
    columns = jnp.zeros((ROWS, LANES), jnp.float32)
    for g, field in enumerate(fields(u_vmem, p_vmem, f_vmem)):
        if g in (0, 1, 4):
            copies[(g + 1) // 2].wait()
        for x in range(OWN):
            lane = g * GROUP + lane_of(x)
            moved = pltpu.roll(field[x], lane + 2 * first, 1)
            columns = jnp.where(pair == lane // 2, moved, columns)
    out_ref[...] = columns


def is_even(axes):
    return lax.rem(lax.axis_index(axes), 2) == 0


def sort_out(even, up, down):
    return jnp.where(even, up, down), jnp.where(even, down, up)


def y_faces(u_ref, f_ref, p_ref, columns_ref, first_ref, second_ref):
    up = [u_ref[:, ROWS - 2, :], u_ref[:, ROWS - 1, :]]
    up += [p_ref[d, :, ROWS - 2, :] for d in range(3)]
    up += [p_ref[d, :, ROWS - 1, :] for d in range(3)]
    up += [f_ref[:, ROWS - 1, :], columns_ref[ROWS - 8 :, :]]
    down = {0: u_ref[:, 0, :], 1: u_ref[:, 1, :], 8: f_ref[:, 0, :], 9: columns_ref[:8, :]}
    down |= {2 + d: p_ref[d, :, 0, :] for d in range(3)}
    even = is_even(GY)
    for k, tile in enumerate(up):
        first_ref[k], second_ref[k] = sort_out(even, tile, down.get(k, tile))


U_ROWS = ((0, False, 0), (1, False, 1), (6, True, 0), (7, True, 1))
P_ROWS = tuple(((0, False, 2 + d), (6, True, 2 + d), (7, True, 5 + d)) for d in range(3))
F_ROWS = ((0, False, 8), (7, True, 8))
HALO_ROWS = (U_ROWS, *P_ROWS, F_ROWS)


class Local:
    def __init__(self):
        self.size_x = OWN * lax.axis_size(GX)
        size_y = ROWS * lax.axis_size(GY)
        self.start_x = lax.axis_index(GX) * OWN
        start_y = lax.axis_index(GY) * ROWS
        self.later = lax.axis_index(GZ).astype(jnp.float32)
        lane = lanes_of(ALL_ROWS)
        row = rows_of(ALL_ROWS)
        self.lane = lane
        self.odd = (lane & 1) == 1
        self.last_lane = lane == LANES - 1
        self.first_lane = lane == 0
        place_y = start_y + jnp.where(row < ROWS + 4, row, row - ALL_ROWS)
        self.inside_y = jnp.where((place_y >= 0) & (place_y <= size_y - 2), 1.0, 0.0)
        self.inside_z = 1.0 - self.later * jnp.where(self.last_lane, 1.0, 0.0)
        place_x = self.start_x + ((lane % GROUP) >> 1) - 2
        self.inside_h = jnp.where((place_x >= 0) & (place_x <= self.size_x - 2), 1.0, 0.0)
        self.columns_inside = (self.inside_h, self.inside_y, 1.0)

    def inside(self, x):
        place = self.start_x + x
        at_x = jnp.where((place >= 0) & (place <= self.size_x - 2), 1.0, 0.0)
        return (at_x, self.inside_y, self.inside_z)

    def columns_at(self, x):
        return (self.lane >> 1) == x + 2

    def following(self, v, columns, x):
        return jnp.where(self.last_lane, from_columns(columns, x), turn(v, -1))

    def preceding(self, v, columns, x):
        return jnp.where(self.first_lane, self.later * from_columns(columns, x), turn(v, 1))

    def columns_following(self, v, gathered):
        return jnp.where(self.odd, gathered, turn(v, -1))

    def columns_preceding(self, v, gathered):
        return jnp.where(self.odd, turn(v, 1), gathered)

    def move(self, dual, bar, nexts, inside):
        return [p + (STEP_DUAL * i) * (n - bar) for p, n, i in zip(dual, nexts, inside)]

    def project(self, moved, inside):
        square = moved[0] * moved[0] + moved[1] * moved[1] + moved[2] * moved[2]
        scale = RADIUS * lax.rsqrt(jnp.maximum(square, RADIUS * RADIUS))
        return [q * (scale * i) for q, i in zip(moved, inside)]

    def dual_plane(self, dual, bar, above, columns_bar, x):
        nexts = (above, next_row(bar), self.following(bar, columns_bar, x))
        inside = self.inside(x)
        return self.project(self.move(dual, bar, nexts, inside), inside)

    def dual_columns(self, dual, bar, gathered):
        moved = self.move(
            dual,
            bar,
            (turn(bar, -2), next_row(bar), self.columns_following(bar, gathered)),
            self.columns_inside,
        )
        return moved, self.project(moved, self.columns_inside)

    def across(self, dual, columns_z, x):
        return dual[1] - previous_row(dual[1]) + dual[2] - self.preceding(dual[2], columns_z, x)

    def columns_across(self, dual, gathered):
        return (
            dual[1] - previous_row(dual[1]) + dual[2] - self.columns_preceding(dual[2], gathered)
        )


UPDATE = 1.0 / (1.0 + STEP_PRIMAL)
BAR_U = 2.0 * UPDATE - 1.0
BAR_F = 2.0 * UPDATE * STEP_PRIMAL


def updated(u, f, divergence):
    return (u + STEP_PRIMAL * (divergence + f)) * UPDATE


def early_bar(u, f):
    return BAR_U * u + BAR_F * f


def fold(v):
    return v[0:8] + v[8:16] + v[16:24] + v[24:32]


def change_of(new, old):
    return sum(fold((n - o) * (n - o)) for n, o in zip(new, old))


def plane_of(u_ref, f_ref, p_ref, halo_ref):
    sources = fields(u_ref, p_ref, f_ref)

    def plane(field, x):
        return jnp.concatenate([sources[field][x], halo_ref[field, x]], axis=0)

    def dual(x):
        return [plane(1 + d, x) for d in range(3)]

    return plane, dual


def split(columns):
    u, p0, p1, p2, f = [turn(columns, -GROUP * g) for g in range(5)]
    return u, [p0, p1, p2], f


def zeros():
    return jnp.zeros((ALL_ROWS, LANES), jnp.float32)


def gather(v, planes):
    into = zeros()
    for x in planes:
        into = into_columns(into, v(x), x)
    return into


def x_faces(
    u_ref, f_ref, p_ref, columns_ref, first_y_ref, second_y_ref,
    halo_ref, columns_out, first_ref, second_ref, below_s, above_s,
):
    even = is_even(GY)
    for k in range(10):
        above_s[k], below_s[k] = sort_out(even, first_y_ref[k], second_y_ref[k])
    for field in range(5):
        for x in range(OWN):
            halo_ref[field, x] = jnp.zeros((8, LANES), jnp.float32)
            for row, from_below, tile in HALO_ROWS[field]:
                source = below_s if from_below else above_s
                halo_ref[field, x, row : row + 1, :] = source[tile, x : x + 1, :]
    row = rows_of(8)
    columns_out[:ROWS, :] = columns_ref[...]
    columns_out[ROWS:, :] = jnp.where(row >= 6, below_s[9], jnp.where(row < 2, above_s[9], 0.0))

    here = Local()
    plane, dual = plane_of(u_ref, f_ref, p_ref, halo_ref)
    c_u, c_p, c_f = split(columns_out[...])
    c_moved, c_dual = here.dual_columns(c_p, c_u, gather(lambda x: plane(0, x), (0, 6, 7)))

    top = OWN - 1
    u, p = plane(0, top), dual(top)
    nexts = (0.0, next_row(u), here.following(u, c_u, top))
    moved = here.move(p, u, nexts, (1.0, here.inside_y, here.inside_z))
    last = here.dual_plane(dual(top - 1), plane(0, top - 1), u, c_u, top - 1)
    up = [*moved, early_bar(u, plane(4, top)) - BAR_F * last[0]]
    c_up = [
        c_p[0] - STEP_DUAL * c_u, c_moved[1], c_moved[2],
        early_bar(c_u, c_f) - BAR_F * turn(c_dual[0], 2),
    ]

    u = plane(0, 0)
    new = here.dual_plane(dual(0), u, plane(0, 1), c_u, 0)
    bar = early_bar(u, plane(4, 0)) + BAR_F * (new[0] + here.across(new, c_dual[2], 0))
    down = [u, bar]
    gathered = into_columns(zeros(), new[2], 0)
    c_bar = early_bar(c_u, c_f) + BAR_F * (c_dual[0] + here.columns_across(c_dual, gathered))
    c_down = [c_u, c_bar]

    def packed(parts):
        group = here.lane // GROUP
        whole = parts[0]
        for k, part in enumerate(parts[1:], 1):
            whole = jnp.where(group == k, turn(part, GROUP * k), whole)
        return whole

    up.append(packed(c_up))
    down = [*down, up[2], up[3], packed(c_down)]
    even = is_even(GX)
    for k in range(5):
        first_ref[k], second_ref[k] = sort_out(even, up[k], down[k])


def early(
    u_ref, f_ref, p_ref, halo_ref, columns_ref,
    dual_out, bar_out, primal_out, dual_end, primal_end, gathered_out, sums_out,
):
    here = Local()
    plane, dual = plane_of(u_ref, f_ref, p_ref, halo_ref)
    c_u, c_p, c_f = split(columns_ref[...])
    sums = [jnp.zeros((8, LANES), jnp.float32) for _ in range(2)]

    gathered_u = gather(lambda x: plane(0, x), range(OWN))
    _, c_dual = here.dual_columns(c_p, c_u, gathered_u)
    gathered_dual = zeros()
    gathered_bar = zeros()
    for x in range(7):
        old = dual(x)
        u = plane(0, x)
        new = here.dual_plane(old, u, plane(0, x + 1), c_u, x)
        sums[0] += change_of(new, old) * (1.0 / STEP_DUAL)
        gathered_dual = into_columns(gathered_dual, new[2], x)
        for d in range(3):
            dual_out[d, x] = new[d]
        if x > 0:
            divergence = new[0] - previous + here.across(new, c_dual[2], x)
            now = updated(u, plane(4, x), divergence)
            bar = 2.0 * now - u
            sums[0] += change_of([now], [u]) * (1.0 / STEP_PRIMAL)
            gathered_bar = into_columns(gathered_bar, bar, x)
            primal_out[x] = now
            bar_out[x] = bar
        previous = new[0]
    divergence = c_dual[0] - turn(c_dual[0], 2) + here.columns_across(c_dual, gathered_dual)
    c_bar = early_bar(c_u, c_f) + BAR_F * divergence

    _, c_end = here.dual_columns(c_dual, c_bar, gathered_bar)
    for x in range(1, 6):
        old = [dual_out[d, x] for d in range(3)]
        new = here.dual_plane(old, bar_out[x], bar_out[x + 1], c_bar, x)
        sums[1] += change_of(new, old) * (1.0 / STEP_DUAL)
        for d in range(3):
            dual_end[d, x] = new[d]
        if x > 1:
            u = primal_out[x]
            divergence = new[0] - previous + here.across(new, c_end[2], x)
            now = updated(u, plane(4, x), divergence)
            sums[1] += change_of([now], [u]) * (1.0 / STEP_PRIMAL)
            primal_end[x] = now[:ROWS]
        previous = new[0]
    for k, v in enumerate((gathered_u, gathered_dual, gathered_bar)):
        gathered_out[k] = v
    for k in range(2):
        sums_out[k] = sums[k]


def late(
    u_ref, f_ref, p_ref, halo_ref, columns_ref, second_x_ref, first_x_ref,
    dual_ref, bar_ref, primal_ref, dual_end, primal_end, gathered_ref, early_sums,
    u_out, p_out, sums_out, u_s, p_s, sem,
):
    copies = []

    def write(source, target):
        copies.append(pltpu.make_async_copy(source, target, sem.at[len(copies)]))
        copies[-1].start()

    write(dual_end.at[:, 1:6, :ROWS], p_out.at[:, 1:6])
    write(primal_end.at[2:6], u_out.at[2:6])
    here = Local()
    plane, dual = plane_of(u_ref, f_ref, p_ref, halo_ref)
    even = is_even(GX)
    above, below = zip(*[sort_out(even, first_x_ref[k], second_x_ref[k]) for k in range(5)])
    sums = [early_sums[0], early_sums[1]]

    c_u, c_p, c_f = split(columns_ref[...])
    lowest, highest = here.columns_at(-1), here.columns_at(OWN)

    def from_below(k):
        return turn(below[4], -GROUP * k - 16)

    def from_above(k):
        return turn(above[4], -GROUP * k + 16)

    c_u = jnp.where(highest, from_above(0), c_u)
    c_moved, _ = here.dual_columns(c_p, c_u, gathered_ref[0])
    sent = (from_below(0) + STEP_DUAL * turn(c_u, -2), from_below(1), from_below(2))
    c_moved = [jnp.where(lowest, s, m) for s, m in zip(sent, c_moved)]
    c_dual = here.project(c_moved, here.columns_inside)

    duals = {x: [dual_ref[d, x] for d in range(3)] for x in range(7)}
    bars = {x: bar_ref[x] for x in range(1, 7)}
    primals = {x: primal_ref[x] for x in range(1, 7)}
    top = OWN - 1
    moved = (below[0] + STEP_DUAL * plane(0, 0), below[1], below[2])
    duals[-1] = here.project(moved, here.inside(-1))
    old = dual(top)
    duals[top] = here.dual_plane(old, plane(0, top), above[0], c_u, top)
    sums[0] += change_of(duals[top], old) * (1.0 / STEP_DUAL)
    for x in (0, top):
        u = plane(0, x)
        divergence = duals[x][0] - duals[x - 1][0] + here.across(duals[x], c_dual[2], x)
        primals[x] = updated(u, plane(4, x), divergence)
        bars[x] = 2.0 * primals[x] - u
        sums[0] += change_of([primals[x]], [u]) * (1.0 / STEP_PRIMAL)
    bars[-1] = below[3] + BAR_F * (duals[-1][0] + here.across(duals[-1], c_dual[2], -1))
    bars[OWN] = above[1] - BAR_F * duals[top][0]

    gathered = gathered_ref[1]
    for x in (-1, top):
        gathered = into_columns(gathered, duals[x][2], x)
    known = jnp.where(
        lowest, from_below(3), jnp.where(highest, from_above(1), early_bar(c_u, c_f))
    )
    own_part = jnp.where(highest, 0.0, c_dual[0] + here.columns_across(c_dual, gathered))
    previous = jnp.where(lowest, 0.0, turn(c_dual[0], 2))
    c_bar = known + BAR_F * (own_part - previous)

    gathered = gathered_ref[2]
    for x in (0, top):
        gathered = into_columns(gathered, bars[x], x)
    _, c_end = here.dual_columns(c_dual, c_bar, gathered)
    ends = {x: [dual_end[d, x] for d in range(3)] for x in range(1, 6)}
    for x in (6, 7, -1, 0):
        ends[x] = here.dual_plane(duals[x], bars[x], bars[x + 1], c_bar, x)
        if x >= 0:
            sums[1] += change_of(ends[x], duals[x]) * (1.0 / STEP_DUAL)
            for d in range(3):
                p_s[d, x] = ends[x][d][:ROWS]
    write(p_s.at[:, 6:8], p_out.at[:, 6:8])
    write(p_s.at[:, 0:1], p_out.at[:, 0:1])
    for x in (6, 7, 0, 1):
        divergence = ends[x][0] - ends[x - 1][0] + here.across(ends[x], c_end[2], x)
        now = updated(primals[x], plane(4, x), divergence)
        sums[1] += change_of([now], [primals[x]]) * (1.0 / STEP_PRIMAL)
        u_s[x] = now[:ROWS]
    write(u_s.at[6:8], u_out.at[6:8])
    write(u_s.at[0:2], u_out.at[0:2])
    out_lane = lanes_of(8)
    sums_out[...] = jnp.where(
        out_lane == 0, jnp.sum(sums[0]), jnp.where(out_lane == 1, jnp.sum(sums[1]), 0.0)
    )
    for copy in copies:
        copy.wait()


def shape(*dims):
    return jax.ShapeDtypeStruct(dims, jnp.float32)


def call(kernel, count, outs, scratch=(), specs=None, out_specs=None, work=0):
    return pl.pallas_call(
        kernel,
        out_shape=outs,
        in_specs=specs or [VMEM] * count,
        out_specs=out_specs or jax.tree.map(lambda _: VMEM, outs),
        scratch_shapes=list(scratch),
        compiler_params=pltpu.CompilerParams(vmem_limit_bytes=4 * 2**20),
        cost_estimate=pl.CostEstimate(flops=work, bytes_accessed=work, transcendentals=0),
    )


def trade(first, second, axes):
    count = lax.axis_size(axes)
    outer = [(i, (i + 1 if i % 2 else i - 1) % count) for i in range(count)]
    second = lax.ppermute(second, axes, outer)
    first = lax.ppermute(first, axes, [(i, i ^ 1) for i in range(count)])
    return first, second


STAGES = ((("core", "y"), 12), (("xl", "z", "xh"), (0 * 8 + 5) * 2 + 1))


def settle(rows):
    values = rows[:1, :2]
    for axes, member in STAGES:
        count = lax.axis_size(axes)
        order = [member] + [i for i in range(count) if i != member]
        spread = jnp.broadcast_to(values, (count, 2))
        spread = lax.all_to_all(spread, axes, 0, 0, tiled=True, axis_index_groups=[order])
        values = jnp.sum(spread, axis=0, keepdims=True)
    return values[0, :2]


def on_device(f, u, p):
    inputs = [pltpu.with_memory_space_constraint(v, pltpu.HBM) for v in (u, f, p)]
    columns, u, f, p = call(
        load,
        3,
        (shape(ROWS, LANES), shape(*u.shape), shape(*f.shape), shape(*p.shape)),
        [pltpu.SemaphoreType.DMA((3,))],
        [HBM] * 3,
    )(*inputs)
    columns = lax.ppermute(columns, GZ, [(0, 1), (1, 0)])

    message = shape(10, 8, LANES)
    first_y, second_y = trade(*call(y_faces, 4, (message, message))(u, f, p, columns), GY)

    message = shape(5, ALL_ROWS, LANES)
    halo, columns, first, second = call(
        x_faces,
        6,
        (shape(5, OWN, 8, LANES), shape(ALL_ROWS, LANES), message, message),
        [pltpu.VMEM((10, 8, LANES), jnp.float32)] * 2,
    )(u, f, p, columns, first_y, second_y)
    first, second = trade(first, second, GX)

    planes = shape(OWN, ALL_ROWS, LANES)
    triple = shape(3, OWN, ALL_ROWS, LANES)
    done = call(
        early,
        5,
        (
            triple, planes, planes, triple, shape(OWN, ROWS, LANES),
            shape(3, ALL_ROWS, LANES), shape(2, 8, LANES),
        ),
        work=10**6,
    )(u, f, p, halo, columns)
    denoised, dual, sums = call(
        late,
        14,
        (shape(OWN, ROWS, LANES), shape(3, OWN, ROWS, LANES), shape(8, LANES)),
        [
            pltpu.VMEM((OWN, ROWS, LANES), jnp.float32),
            pltpu.VMEM((3, OWN, ROWS, LANES), jnp.float32),
            pltpu.SemaphoreType.DMA((6,)),
        ],
        out_specs=(HBM, HBM, VMEM),
    )(u, f, p, halo, columns, second, first, *done)
    cells = OWN * lax.axis_size(GX) * ROWS * lax.axis_size(GY) * LANES * lax.axis_size(GZ)
    return denoised, dual, jnp.sqrt(settle(sums) / float(cells))


def solution(mesh):
    mesh = Mesh(mesh.devices.reshape(SIZES), ("xl", "z", "core", "y", "xh"))
    placed = (P(GX, GY, GZ), P(GX, GY, GZ), P(None, GX, GY, GZ))
    return jax.shard_map(
        on_device,
        mesh=mesh,
        in_specs=placed,
        out_specs=(P(GX, GY, GZ), P(None, GX, GY, GZ), P()),
        check_vma=False,
    )
```

```python
import jax
import jax.numpy as jnp
from jax import lax
from jax.experimental import pallas as pl
from jax.experimental.pallas import tpu as pltpu
from jax.sharding import Mesh, PartitionSpec as P


GX = ("xl", "z", "core")
GY = "y"
GZ = "xh"
SIZES = (2, 8, 2, 8, 2)

STEP_PRIMAL = 0.25
STEP_DUAL = 0.3
RADIUS = 0.5
OWN = 8
ROWS = 32
ALL_ROWS = 40
LANES = 128
GROUP = 24

VMEM = pl.BlockSpec(memory_space=pltpu.VMEM)


def lanes_of(rows):
    return lax.broadcasted_iota(jnp.int32, (rows, LANES), 1)


def rows_of(rows):
    return lax.broadcasted_iota(jnp.int32, (rows, LANES), 0)


def fields(u_ref, p_ref, f_ref):
    return (u_ref, p_ref.at[0], p_ref.at[1], p_ref.at[2], f_ref)


def next_row(v):
    return pltpu.roll(v, v.shape[0] - 1, 0)


def previous_row(v):
    return pltpu.roll(v, 1, 0)


def turn(v, by):
    return pltpu.roll(v, by % LANES, 1)


def lane_of(x):
    return 2 * (x + 2)


def from_columns(v, x):
    return turn(v, LANES - 1 - lane_of(x))


def into_columns(into, v, x):
    return jnp.where((lanes_of(ALL_ROWS) >> 1) == x + 2, turn(v, lane_of(x) + 1), into)


def load(u_ref, f_ref, p_ref, out_ref, u_vmem, f_vmem, p_vmem, sem):
    arrays = ((u_ref, u_vmem), (p_ref, p_vmem), (f_ref, f_vmem))
    copies = [pltpu.make_async_copy(a, b, sem.at[k]) for k, (a, b) in enumerate(arrays)]
    for copy in copies:
        copy.start()
    first = 1 - lax.axis_index(GZ)
    pair = lanes_of(ROWS) >> 1
    columns = jnp.zeros((ROWS, LANES), jnp.float32)
    for g, field in enumerate(fields(u_vmem, p_vmem, f_vmem)):
        if g in (0, 1, 4):
            copies[(g + 1) // 2].wait()
        for x in range(OWN):
            lane = g * GROUP + lane_of(x)
            moved = pltpu.roll(field[x], lane + 2 * first, 1)
            columns = jnp.where(pair == lane // 2, moved, columns)
    out_ref[...] = columns


def is_even(axes):
    return lax.rem(lax.axis_index(axes), 2) == 0


def sort_out(even, up, down):
    return jnp.where(even, up, down), jnp.where(even, down, up)


def y_faces(u_ref, f_ref, p_ref, columns_ref, first_ref, second_ref):
    up = [u_ref[:, ROWS - 2, :], u_ref[:, ROWS - 1, :]]
    up += [p_ref[d, :, ROWS - 2, :] for d in range(3)]
    up += [p_ref[d, :, ROWS - 1, :] for d in range(3)]
    up += [f_ref[:, ROWS - 1, :], columns_ref[ROWS - 8 :, :]]
    down = {0: u_ref[:, 0, :], 1: u_ref[:, 1, :], 8: f_ref[:, 0, :], 9: columns_ref[:8, :]}
    down |= {2 + d: p_ref[d, :, 0, :] for d in range(3)}
    even = is_even(GY)
    for k, tile in enumerate(up):
        first_ref[k], second_ref[k] = sort_out(even, tile, down.get(k, tile))


U_ROWS = ((0, False, 0), (1, False, 1), (6, True, 0), (7, True, 1))
P_ROWS = tuple(((0, False, 2 + d), (6, True, 2 + d), (7, True, 5 + d)) for d in range(3))
F_ROWS = ((0, False, 8), (7, True, 8))
HALO_ROWS = (U_ROWS, *P_ROWS, F_ROWS)


class Local:
    def __init__(self):
        self.size_x = OWN * lax.axis_size(GX)
        size_y = ROWS * lax.axis_size(GY)
        self.start_x = lax.axis_index(GX) * OWN
        start_y = lax.axis_index(GY) * ROWS
        self.later = lax.axis_index(GZ).astype(jnp.float32)
        lane = lanes_of(ALL_ROWS)
        row = rows_of(ALL_ROWS)
        self.lane = lane
        self.odd = (lane & 1) == 1
        self.last_lane = lane == LANES - 1
        self.first_lane = lane == 0
        place_y = start_y + jnp.where(row < ROWS + 4, row, row - ALL_ROWS)
        self.inside_y = jnp.where((place_y >= 0) & (place_y <= size_y - 2), 1.0, 0.0)
        self.inside_z = 1.0 - self.later * jnp.where(self.last_lane, 1.0, 0.0)
        place_x = self.start_x + ((lane % GROUP) >> 1) - 2
        self.inside_h = jnp.where((place_x >= 0) & (place_x <= self.size_x - 2), 1.0, 0.0)
        self.columns_inside = (self.inside_h, self.inside_y, 1.0)

    def inside(self, x):
        place = self.start_x + x
        at_x = jnp.where((place >= 0) & (place <= self.size_x - 2), 1.0, 0.0)
        return (at_x, self.inside_y, self.inside_z)

    def columns_at(self, x):
        return (self.lane >> 1) == x + 2

    def following(self, v, columns, x):
        return jnp.where(self.last_lane, from_columns(columns, x), turn(v, -1))

    def preceding(self, v, columns, x):
        return jnp.where(self.first_lane, self.later * from_columns(columns, x), turn(v, 1))

    def columns_following(self, v, gathered):
        return jnp.where(self.odd, gathered, turn(v, -1))

    def columns_preceding(self, v, gathered):
        return jnp.where(self.odd, turn(v, 1), gathered)

    def move(self, dual, bar, nexts, inside):
        return [p + (STEP_DUAL * i) * (n - bar) for p, n, i in zip(dual, nexts, inside)]

    def project(self, moved, inside):
        square = moved[0] * moved[0] + moved[1] * moved[1] + moved[2] * moved[2]
        scale = RADIUS * lax.rsqrt(jnp.maximum(square, RADIUS * RADIUS))
        return [q * (scale * i) for q, i in zip(moved, inside)]

    def dual_plane(self, dual, bar, above, columns_bar, x):
        nexts = (above, next_row(bar), self.following(bar, columns_bar, x))
        inside = self.inside(x)
        return self.project(self.move(dual, bar, nexts, inside), inside)

    def dual_columns(self, dual, bar, gathered):
        moved = self.move(
            dual,
            bar,
            (turn(bar, -2), next_row(bar), self.columns_following(bar, gathered)),
            self.columns_inside,
        )
        return moved, self.project(moved, self.columns_inside)

    def across(self, dual, columns_z, x):
        return dual[1] - previous_row(dual[1]) + dual[2] - self.preceding(dual[2], columns_z, x)

    def columns_across(self, dual, gathered):
        return (
            dual[1] - previous_row(dual[1]) + dual[2] - self.columns_preceding(dual[2], gathered)
        )


UPDATE = 1.0 / (1.0 + STEP_PRIMAL)
BAR_U = 2.0 * UPDATE - 1.0
BAR_F = 2.0 * UPDATE * STEP_PRIMAL


def updated(u, f, divergence):
    return (u + STEP_PRIMAL * (divergence + f)) * UPDATE


def early_bar(u, f):
    return BAR_U * u + BAR_F * f


def fold(v):
    return v[0:8] + v[8:16] + v[16:24] + v[24:32]


def change_of(new, old):
    return sum(fold((n - o) * (n - o)) for n, o in zip(new, old))


def plane_of(u_ref, f_ref, p_ref, halo_ref):
    sources = fields(u_ref, p_ref, f_ref)

    def plane(field, x):
        return jnp.concatenate([sources[field][x], halo_ref[field, x]], axis=0)

    def dual(x):
        return [plane(1 + d, x) for d in range(3)]

    return plane, dual


def split(columns):
    u, p0, p1, p2, f = [turn(columns, -GROUP * g) for g in range(5)]
    return u, [p0, p1, p2], f


def zeros():
    return jnp.zeros((ALL_ROWS, LANES), jnp.float32)


def gather(v, planes):
    into = zeros()
    for x in planes:
        into = into_columns(into, v(x), x)
    return into


def x_faces(
    u_ref, f_ref, p_ref, columns_ref, second_y_ref, first_y_ref,
    halo_ref, columns_out, first_ref, second_ref, below_s, above_s,
):
    even = is_even(GY)
    for k in range(10):
        above_s[k], below_s[k] = sort_out(even, first_y_ref[k], second_y_ref[k])
    for field in range(5):
        for x in range(OWN):
            halo_ref[field, x] = jnp.zeros((8, LANES), jnp.float32)
            for row, from_below, tile in HALO_ROWS[field]:
                source = below_s if from_below else above_s
                halo_ref[field, x, row : row + 1, :] = source[tile, x : x + 1, :]
    row = rows_of(8)
    columns_out[:ROWS, :] = columns_ref[...]
    columns_out[ROWS:, :] = jnp.where(row >= 6, below_s[9], jnp.where(row < 2, above_s[9], 0.0))

    here = Local()
    plane, dual = plane_of(u_ref, f_ref, p_ref, halo_ref)
    c_u, c_p, c_f = split(columns_out[...])
    c_moved, c_dual = here.dual_columns(c_p, c_u, gather(lambda x: plane(0, x), (0, 6, 7)))

    top = OWN - 1
    u, p = plane(0, top), dual(top)
    nexts = (0.0, next_row(u), here.following(u, c_u, top))
    moved = here.move(p, u, nexts, (1.0, here.inside_y, here.inside_z))
    last = here.dual_plane(dual(top - 1), plane(0, top - 1), u, c_u, top - 1)
    up = [*moved, early_bar(u, plane(4, top)) - BAR_F * last[0]]
    c_up = [
        c_p[0] - STEP_DUAL * c_u, c_moved[1], c_moved[2],
        early_bar(c_u, c_f) - BAR_F * turn(c_dual[0], 2),
    ]

    u = plane(0, 0)
    new = here.dual_plane(dual(0), u, plane(0, 1), c_u, 0)
    bar = early_bar(u, plane(4, 0)) + BAR_F * (new[0] + here.across(new, c_dual[2], 0))
    down = [u, bar]
    gathered = into_columns(zeros(), new[2], 0)
    c_bar = early_bar(c_u, c_f) + BAR_F * (c_dual[0] + here.columns_across(c_dual, gathered))
    c_down = [c_u, c_bar]

    def packed(parts):
        group = here.lane // GROUP
        whole = parts[0]
        for k, part in enumerate(parts[1:], 1):
            whole = jnp.where(group == k, turn(part, GROUP * k), whole)
        return whole

    up.append(packed(c_up))
    down = [*down, up[2], up[3], packed(c_down)]
    even = is_even(GX)
    for k in range(5):
        first_ref[k], second_ref[k] = sort_out(even, up[k], down[k])


def early(
    u_ref, f_ref, p_ref, halo_ref, columns_ref,
    dual_out, bar_out, primal_out, dual_end, primal_end, gathered_out, sums_out,
):
    here = Local()
    plane, dual = plane_of(u_ref, f_ref, p_ref, halo_ref)
    c_u, c_p, c_f = split(columns_ref[...])
    sums = [jnp.zeros((8, LANES), jnp.float32) for _ in range(2)]

    gathered_u = gather(lambda x: plane(0, x), range(OWN))
    _, c_dual = here.dual_columns(c_p, c_u, gathered_u)
    gathered_dual = zeros()
    gathered_bar = zeros()
    for x in range(7):
        old = dual(x)
        u = plane(0, x)
        new = here.dual_plane(old, u, plane(0, x + 1), c_u, x)
        sums[0] += change_of(new, old) * (1.0 / STEP_DUAL)
        gathered_dual = into_columns(gathered_dual, new[2], x)
        for d in range(3):
            dual_out[d, x] = new[d]
        if x > 0:
            divergence = new[0] - previous + here.across(new, c_dual[2], x)
            now = updated(u, plane(4, x), divergence)
            bar = 2.0 * now - u
            sums[0] += change_of([now], [u]) * (1.0 / STEP_PRIMAL)
            gathered_bar = into_columns(gathered_bar, bar, x)
            primal_out[x] = now
            bar_out[x] = bar
        previous = new[0]
    divergence = c_dual[0] - turn(c_dual[0], 2) + here.columns_across(c_dual, gathered_dual)
    c_bar = early_bar(c_u, c_f) + BAR_F * divergence

    _, c_end = here.dual_columns(c_dual, c_bar, gathered_bar)
    for x in range(1, 6):
        old = [dual_out[d, x] for d in range(3)]
        new = here.dual_plane(old, bar_out[x], bar_out[x + 1], c_bar, x)
        sums[1] += change_of(new, old) * (1.0 / STEP_DUAL)
        for d in range(3):
            dual_end[d, x] = new[d]
        if x > 1:
            u = primal_out[x]
            divergence = new[0] - previous + here.across(new, c_end[2], x)
            now = updated(u, plane(4, x), divergence)
            sums[1] += change_of([now], [u]) * (1.0 / STEP_PRIMAL)
            primal_end[x] = now[:ROWS]
        previous = new[0]
    for k, v in enumerate((gathered_u, gathered_dual, gathered_bar)):
        gathered_out[k] = v
    for k in range(2):
        sums_out[k] = sums[k]


def late(
    u_ref, f_ref, p_ref, halo_ref, columns_ref, second_x_ref, first_x_ref,
    dual_ref, bar_ref, primal_ref, dual_end, primal_end, gathered_ref, early_sums,
    u_out, p_out, sums_out,
):
    here = Local()
    plane, dual = plane_of(u_ref, f_ref, p_ref, halo_ref)
    even = is_even(GX)
    above, below = zip(*[sort_out(even, first_x_ref[k], second_x_ref[k]) for k in range(5)])
    sums = [early_sums[0], early_sums[1]]

    c_u, c_p, c_f = split(columns_ref[...])
    lowest, highest = here.columns_at(-1), here.columns_at(OWN)

    def from_below(k):
        return turn(below[4], -GROUP * k - 16)

    def from_above(k):
        return turn(above[4], -GROUP * k + 16)

    c_u = jnp.where(highest, from_above(0), c_u)
    c_moved, _ = here.dual_columns(c_p, c_u, gathered_ref[0])
    sent = (from_below(0) + STEP_DUAL * turn(c_u, -2), from_below(1), from_below(2))
    c_moved = [jnp.where(lowest, s, m) for s, m in zip(sent, c_moved)]
    c_dual = here.project(c_moved, here.columns_inside)

    duals = {x: [dual_ref[d, x] for d in range(3)] for x in range(7)}
    bars = {x: bar_ref[x] for x in range(1, 7)}
    primals = {x: primal_ref[x] for x in range(1, 7)}
    top = OWN - 1
    moved = (below[0] + STEP_DUAL * plane(0, 0), below[1], below[2])
    duals[-1] = here.project(moved, here.inside(-1))
    old = dual(top)
    duals[top] = here.dual_plane(old, plane(0, top), above[0], c_u, top)
    sums[0] += change_of(duals[top], old) * (1.0 / STEP_DUAL)
    for x in (0, top):
        u = plane(0, x)
        divergence = duals[x][0] - duals[x - 1][0] + here.across(duals[x], c_dual[2], x)
        primals[x] = updated(u, plane(4, x), divergence)
        bars[x] = 2.0 * primals[x] - u
        sums[0] += change_of([primals[x]], [u]) * (1.0 / STEP_PRIMAL)
    bars[-1] = below[3] + BAR_F * (duals[-1][0] + here.across(duals[-1], c_dual[2], -1))
    bars[OWN] = above[1] - BAR_F * duals[top][0]

    gathered = gathered_ref[1]
    for x in (-1, top):
        gathered = into_columns(gathered, duals[x][2], x)
    known = jnp.where(
        lowest, from_below(3), jnp.where(highest, from_above(1), early_bar(c_u, c_f))
    )
    own_part = jnp.where(highest, 0.0, c_dual[0] + here.columns_across(c_dual, gathered))
    previous = jnp.where(lowest, 0.0, turn(c_dual[0], 2))
    c_bar = known + BAR_F * (own_part - previous)

    gathered = gathered_ref[2]
    for x in (0, top):
        gathered = into_columns(gathered, bars[x], x)
    _, c_end = here.dual_columns(c_dual, c_bar, gathered)
    ends = {x: [dual_end[d, x] for d in range(3)] for x in range(1, 6)}
    for x in (-1, 0, 6, 7):
        ends[x] = here.dual_plane(duals[x], bars[x], bars[x + 1], c_bar, x)
        if x >= 0:
            sums[1] += change_of(ends[x], duals[x]) * (1.0 / STEP_DUAL)
    for x in range(OWN):
        if 2 <= x <= 5:
            u_out[x] = primal_end[x]
        else:
            divergence = ends[x][0] - ends[x - 1][0] + here.across(ends[x], c_end[2], x)
            now = updated(primals[x], plane(4, x), divergence)
            sums[1] += change_of([now], [primals[x]]) * (1.0 / STEP_PRIMAL)
            u_out[x] = now[:ROWS]
        for d in range(3):
            p_out[d, x] = ends[x][d][:ROWS]
    for k in range(2):
        total = jnp.sum(sums[k], axis=0, keepdims=True)
        sums_out[:, k * LANES : (k + 1) * LANES] = jnp.broadcast_to(total, (8, LANES))


def shape(*dims):
    return jax.ShapeDtypeStruct(dims, jnp.float32)


def call(kernel, count, outs, scratch=(), specs=None, work=0):
    return pl.pallas_call(
        kernel,
        out_shape=outs,
        in_specs=specs or [VMEM] * count,
        out_specs=jax.tree.map(lambda _: VMEM, outs),
        scratch_shapes=list(scratch),
        compiler_params=pltpu.CompilerParams(vmem_limit_bytes=4 * 2**20),
        cost_estimate=pl.CostEstimate(flops=work, bytes_accessed=work, transcendentals=0),
    )


def trade(first, second, axes):
    count = lax.axis_size(axes)
    outer = [(i, (i + 1 if i % 2 else i - 1) % count) for i in range(count)]
    second = lax.ppermute(second, axes, outer)
    first = lax.ppermute(first, axes, [(i, i ^ 1) for i in range(count)])
    return first, second


STAGES = ((("core", "y"), 12), (("xl", "z", "xh"), (0 * 8 + 5) * 2 + 1))


def settle(rows):
    values = rows[:1]
    for axes, member in STAGES:
        count = lax.axis_size(axes)
        order = [member] + [i for i in range(count) if i != member]
        spread = jnp.broadcast_to(values, (count, 2 * LANES))
        spread = lax.all_to_all(spread, axes, 0, 0, tiled=True, axis_index_groups=[order])
        values = jnp.sum(spread, axis=0, keepdims=True)
    return jnp.sum(values.reshape(2, LANES), axis=1)


def on_device(f, u, p):
    inputs = [pltpu.with_memory_space_constraint(v, pltpu.HBM) for v in (u, f, p)]
    columns, u, f, p = call(
        load,
        3,
        (shape(ROWS, LANES), shape(*u.shape), shape(*f.shape), shape(*p.shape)),
        [pltpu.SemaphoreType.DMA((3,))],
        [pl.BlockSpec(memory_space=pltpu.HBM)] * 3,
    )(*inputs)
    columns = lax.ppermute(columns, GZ, [(0, 1), (1, 0)])

    message = shape(10, 8, LANES)
    first_y, second_y = trade(*call(y_faces, 4, (message, message))(u, f, p, columns), GY)

    message = shape(5, ALL_ROWS, LANES)
    halo, columns, first, second = call(
        x_faces,
        6,
        (shape(5, OWN, 8, LANES), shape(ALL_ROWS, LANES), message, message),
        [pltpu.VMEM((10, 8, LANES), jnp.float32)] * 2,
    )(u, f, p, columns, second_y, first_y)
    first, second = trade(first, second, GX)

    planes = shape(OWN, ALL_ROWS, LANES)
    triple = shape(3, OWN, ALL_ROWS, LANES)
    done = call(
        early,
        5,
        (
            triple, planes, planes, triple, shape(OWN, ROWS, LANES),
            shape(3, ALL_ROWS, LANES), shape(2, 8, LANES),
        ),
        work=10**6,
    )(u, f, p, halo, columns)
    denoised, dual, sums = call(
        late,
        14,
        (shape(OWN, ROWS, LANES), shape(3, OWN, ROWS, LANES), shape(8, 2 * LANES)),
    )(u, f, p, halo, columns, second, first, *done)
    cells = OWN * lax.axis_size(GX) * ROWS * lax.axis_size(GY) * LANES * lax.axis_size(GZ)
    return denoised, dual, jnp.sqrt(settle(sums) / float(cells))


def solution(mesh):
    mesh = Mesh(mesh.devices.reshape(SIZES), ("xl", "z", "core", "y", "xh"))
    placed = (P(GX, GY, GZ), P(GX, GY, GZ), P(None, GX, GY, GZ))
    return jax.shard_map(
        on_device,
        mesh=mesh,
        in_specs=placed,
        out_specs=(P(GX, GY, GZ), P(None, GX, GY, GZ), P()),
        check_vma=False,
    )
```

```python
import jax
import jax.numpy as jnp
from jax import lax
from jax.experimental import pallas as pl
from jax.experimental.pallas import tpu as pltpu
from jax.sharding import Mesh, PartitionSpec as P


GX = ("xl", "z", "core")
GY = "y"
GZ = "xh"
SIZES = (2, 8, 2, 8, 2)

STEP_PRIMAL = 0.25
STEP_DUAL = 0.3
RADIUS = 0.5
OWN = 8
ROWS = 32
ALL_ROWS = 40
LANES = 128
GROUP = 24

VMEM = pl.BlockSpec(memory_space=pltpu.VMEM)


def lanes_of(rows):
    return lax.broadcasted_iota(jnp.int32, (rows, LANES), 1)


def rows_of(rows):
    return lax.broadcasted_iota(jnp.int32, (rows, LANES), 0)


def fields(u_ref, p_ref, f_ref):
    return (u_ref, p_ref.at[0], p_ref.at[1], p_ref.at[2], f_ref)


def next_row(v):
    return pltpu.roll(v, v.shape[0] - 1, 0)


def previous_row(v):
    return pltpu.roll(v, 1, 0)


def turn(v, by):
    return pltpu.roll(v, by % LANES, 1)


def lane_of(x):
    return 2 * (x + 2)


def from_columns(v, x):
    return turn(v, LANES - 1 - lane_of(x))


def into_columns(into, v, x):
    return jnp.where((lanes_of(ALL_ROWS) >> 1) == x + 2, turn(v, lane_of(x) + 1), into)


def load(u_ref, f_ref, p_ref, out_ref, u_vmem, f_vmem, p_vmem, sem):
    arrays = ((u_ref, u_vmem), (p_ref, p_vmem), (f_ref, f_vmem))
    copies = [pltpu.make_async_copy(a, b, sem.at[k]) for k, (a, b) in enumerate(arrays)]
    for copy in copies:
        copy.start()
    first = 1 - lax.axis_index(GZ)
    pair = lanes_of(ROWS) >> 1
    columns = jnp.zeros((ROWS, LANES), jnp.float32)
    for g, field in enumerate(fields(u_vmem, p_vmem, f_vmem)):
        if g in (0, 1, 4):
            copies[(g + 1) // 2].wait()
        for x in range(OWN):
            lane = g * GROUP + lane_of(x)
            moved = pltpu.roll(field[x], lane + 2 * first, 1)
            columns = jnp.where(pair == lane // 2, moved, columns)
    out_ref[...] = columns


def is_even(axes):
    return lax.rem(lax.axis_index(axes), 2) == 0


def sort_out(even, up, down):
    return jnp.where(even, up, down), jnp.where(even, down, up)


def y_faces(u_ref, f_ref, p_ref, columns_ref, first_ref, second_ref):
    up = [u_ref[:, ROWS - 2, :], u_ref[:, ROWS - 1, :]]
    up += [p_ref[d, :, ROWS - 2, :] for d in range(3)]
    up += [p_ref[d, :, ROWS - 1, :] for d in range(3)]
    up += [f_ref[:, ROWS - 1, :], columns_ref[ROWS - 8 :, :]]
    down = {0: u_ref[:, 0, :], 1: u_ref[:, 1, :], 8: f_ref[:, 0, :], 9: columns_ref[:8, :]}
    down |= {2 + d: p_ref[d, :, 0, :] for d in range(3)}
    even = is_even(GY)
    for k, tile in enumerate(up):
        first_ref[k], second_ref[k] = sort_out(even, tile, down.get(k, tile))


U_ROWS = ((0, False, 0), (1, False, 1), (6, True, 0), (7, True, 1))
P_ROWS = tuple(((0, False, 2 + d), (6, True, 2 + d), (7, True, 5 + d)) for d in range(3))
F_ROWS = ((0, False, 8), (7, True, 8))
HALO_ROWS = (U_ROWS, *P_ROWS, F_ROWS)


class Local:
    def __init__(self):
        self.size_x = OWN * lax.axis_size(GX)
        size_y = ROWS * lax.axis_size(GY)
        self.start_x = lax.axis_index(GX) * OWN
        start_y = lax.axis_index(GY) * ROWS
        self.later = lax.axis_index(GZ).astype(jnp.float32)
        lane = lanes_of(ALL_ROWS)
        row = rows_of(ALL_ROWS)
        self.lane = lane
        self.odd = (lane & 1) == 1
        self.last_lane = lane == LANES - 1
        self.first_lane = lane == 0
        place_y = start_y + jnp.where(row < ROWS + 4, row, row - ALL_ROWS)
        self.inside_y = jnp.where((place_y >= 0) & (place_y <= size_y - 2), 1.0, 0.0)
        self.inside_z = 1.0 - self.later * jnp.where(self.last_lane, 1.0, 0.0)
        place_x = self.start_x + ((lane % GROUP) >> 1) - 2
        self.inside_h = jnp.where((place_x >= 0) & (place_x <= self.size_x - 2), 1.0, 0.0)
        self.columns_inside = (self.inside_h, self.inside_y, 1.0)

    def inside(self, x):
        place = self.start_x + x
        at_x = jnp.where((place >= 0) & (place <= self.size_x - 2), 1.0, 0.0)
        return (at_x, self.inside_y, self.inside_z)

    def columns_at(self, x):
        return (self.lane >> 1) == x + 2

    def following(self, v, columns, x):
        return jnp.where(self.last_lane, from_columns(columns, x), turn(v, -1))

    def preceding(self, v, columns, x):
        return jnp.where(self.first_lane, self.later * from_columns(columns, x), turn(v, 1))

    def columns_following(self, v, gathered):
        return jnp.where(self.odd, gathered, turn(v, -1))

    def columns_preceding(self, v, gathered):
        return jnp.where(self.odd, turn(v, 1), gathered)

    def move(self, dual, bar, nexts, inside):
        return [p + (STEP_DUAL * i) * (n - bar) for p, n, i in zip(dual, nexts, inside)]

    def project(self, moved, inside):
        square = moved[0] * moved[0] + moved[1] * moved[1] + moved[2] * moved[2]
        scale = RADIUS * lax.rsqrt(jnp.maximum(square, RADIUS * RADIUS))
        return [q * (scale * i) for q, i in zip(moved, inside)]

    def dual_plane(self, dual, bar, above, columns_bar, x):
        nexts = (above, next_row(bar), self.following(bar, columns_bar, x))
        inside = self.inside(x)
        return self.project(self.move(dual, bar, nexts, inside), inside)

    def dual_columns(self, dual, bar, gathered):
        moved = self.move(
            dual,
            bar,
            (turn(bar, -2), next_row(bar), self.columns_following(bar, gathered)),
            self.columns_inside,
        )
        return moved, self.project(moved, self.columns_inside)

    def across(self, dual, columns_z, x):
        return dual[1] - previous_row(dual[1]) + dual[2] - self.preceding(dual[2], columns_z, x)

    def columns_across(self, dual, gathered):
        return (
            dual[1] - previous_row(dual[1]) + dual[2] - self.columns_preceding(dual[2], gathered)
        )


UPDATE = 1.0 / (1.0 + STEP_PRIMAL)
BAR_U = 2.0 * UPDATE - 1.0
BAR_F = 2.0 * UPDATE * STEP_PRIMAL


def updated(u, f, divergence):
    return (u + STEP_PRIMAL * (divergence + f)) * UPDATE


def early_bar(u, f):
    return BAR_U * u + BAR_F * f


def fold(v):
    return v[0:8] + v[8:16] + v[16:24] + v[24:32]


def change_of(new, old):
    return sum(fold((n - o) * (n - o)) for n, o in zip(new, old))


def plane_of(u_ref, f_ref, p_ref, halo_ref):
    sources = fields(u_ref, p_ref, f_ref)

    def plane(field, x):
        return jnp.concatenate([sources[field][x], halo_ref[field, x]], axis=0)

    def dual(x):
        return [plane(1 + d, x) for d in range(3)]

    return plane, dual


def split(columns):
    u, p0, p1, p2, f = [turn(columns, -GROUP * g) for g in range(5)]
    return u, [p0, p1, p2], f


def zeros():
    return jnp.zeros((ALL_ROWS, LANES), jnp.float32)


def gather(v, planes):
    into = zeros()
    for x in planes:
        into = into_columns(into, v(x), x)
    return into


def lay_out(first_ref, second_ref, halo_ref, below_s, above_s, planes):
    even = is_even(GY)
    for k in range(10):
        above_s[k], below_s[k] = sort_out(even, first_ref[k], second_ref[k])
    for field in range(5):
        for x in planes:
            halo_ref[field, x] = jnp.zeros((8, LANES), jnp.float32)
            for row, from_below, tile in HALO_ROWS[field]:
                source = below_s if from_below else above_s
                halo_ref[field, x, row : row + 1, :] = source[tile, x : x + 1, :]


def x_faces(
    u_ref, f_ref, p_ref, columns_ref, second_y_ref, first_y_ref,
    halo_ref, columns_out, first_ref, second_ref, below_s, above_s,
):
    lay_out(first_y_ref, second_y_ref, halo_ref, below_s, above_s, (0, 1, 6, 7))
    row = rows_of(8)
    columns_out[:ROWS, :] = columns_ref[...]
    columns_out[ROWS:, :] = jnp.where(row >= 6, below_s[9], jnp.where(row < 2, above_s[9], 0.0))

    here = Local()
    plane, dual = plane_of(u_ref, f_ref, p_ref, halo_ref)
    c_u, c_p, c_f = split(columns_out[...])
    c_moved, c_dual = here.dual_columns(c_p, c_u, gather(lambda x: plane(0, x), (0, 6, 7)))

    top = OWN - 1
    u, p = plane(0, top), dual(top)
    nexts = (0.0, next_row(u), here.following(u, c_u, top))
    moved = here.move(p, u, nexts, (1.0, here.inside_y, here.inside_z))
    last = here.dual_plane(dual(top - 1), plane(0, top - 1), u, c_u, top - 1)
    up = [*moved, early_bar(u, plane(4, top)) - BAR_F * last[0]]
    c_up = [
        c_p[0] - STEP_DUAL * c_u, c_moved[1], c_moved[2],
        early_bar(c_u, c_f) - BAR_F * turn(c_dual[0], 2),
    ]

    u = plane(0, 0)
    new = here.dual_plane(dual(0), u, plane(0, 1), c_u, 0)
    bar = early_bar(u, plane(4, 0)) + BAR_F * (new[0] + here.across(new, c_dual[2], 0))
    down = [u, bar]
    gathered = into_columns(zeros(), new[2], 0)
    c_bar = early_bar(c_u, c_f) + BAR_F * (c_dual[0] + here.columns_across(c_dual, gathered))
    c_down = [c_u, c_bar]

    def packed(parts):
        group = here.lane // GROUP
        whole = parts[0]
        for k, part in enumerate(parts[1:], 1):
            whole = jnp.where(group == k, turn(part, GROUP * k), whole)
        return whole

    up.append(packed(c_up))
    down = [*down, up[2], up[3], packed(c_down)]
    even = is_even(GX)
    for k in range(5):
        first_ref[k], second_ref[k] = sort_out(even, up[k], down[k])


def early(
    u_ref, f_ref, p_ref, columns_ref, first_y_ref, second_y_ref,
    dual_out, bar_out, primal_out, dual_end, primal_end, gathered_out, sums_out,
    halo_ref, below_s, above_s,
):
    lay_out(first_y_ref, second_y_ref, halo_ref, below_s, above_s, range(OWN))
    here = Local()
    plane, dual = plane_of(u_ref, f_ref, p_ref, halo_ref)
    c_u, c_p, c_f = split(columns_ref[...])
    sums = [jnp.zeros((8, LANES), jnp.float32) for _ in range(2)]

    gathered_u = gather(lambda x: plane(0, x), range(OWN))
    _, c_dual = here.dual_columns(c_p, c_u, gathered_u)
    gathered_dual = zeros()
    gathered_bar = zeros()
    for x in range(7):
        old = dual(x)
        u = plane(0, x)
        new = here.dual_plane(old, u, plane(0, x + 1), c_u, x)
        sums[0] += change_of(new, old) * (1.0 / STEP_DUAL)
        gathered_dual = into_columns(gathered_dual, new[2], x)
        for d in range(3):
            dual_out[d, x] = new[d]
        if x > 0:
            divergence = new[0] - previous + here.across(new, c_dual[2], x)
            now = updated(u, plane(4, x), divergence)
            bar = 2.0 * now - u
            sums[0] += change_of([now], [u]) * (1.0 / STEP_PRIMAL)
            gathered_bar = into_columns(gathered_bar, bar, x)
            primal_out[x] = now
            bar_out[x] = bar
        previous = new[0]
    divergence = c_dual[0] - turn(c_dual[0], 2) + here.columns_across(c_dual, gathered_dual)
    c_bar = early_bar(c_u, c_f) + BAR_F * divergence

    _, c_end = here.dual_columns(c_dual, c_bar, gathered_bar)
    for x in range(1, 6):
        old = [dual_out[d, x] for d in range(3)]
        new = here.dual_plane(old, bar_out[x], bar_out[x + 1], c_bar, x)
        sums[1] += change_of(new, old) * (1.0 / STEP_DUAL)
        for d in range(3):
            dual_end[d, x] = new[d]
        if x > 1:
            u = primal_out[x]
            divergence = new[0] - previous + here.across(new, c_end[2], x)
            now = updated(u, plane(4, x), divergence)
            sums[1] += change_of([now], [u]) * (1.0 / STEP_PRIMAL)
            primal_end[x] = now[:ROWS]
        previous = new[0]
    for k, v in enumerate((gathered_u, gathered_dual, gathered_bar)):
        gathered_out[k] = v
    for k in range(2):
        sums_out[k] = sums[k]


def late(
    u_ref, f_ref, p_ref, halo_ref, columns_ref, second_x_ref, first_x_ref,
    dual_ref, bar_ref, primal_ref, dual_end, primal_end, gathered_ref, early_sums,
    u_out, p_out, sums_out,
):
    here = Local()
    plane, dual = plane_of(u_ref, f_ref, p_ref, halo_ref)
    even = is_even(GX)
    above, below = zip(*[sort_out(even, first_x_ref[k], second_x_ref[k]) for k in range(5)])
    sums = [early_sums[0], early_sums[1]]

    c_u, c_p, c_f = split(columns_ref[...])
    lowest, highest = here.columns_at(-1), here.columns_at(OWN)

    def from_below(k):
        return turn(below[4], -GROUP * k - 16)

    def from_above(k):
        return turn(above[4], -GROUP * k + 16)

    c_u = jnp.where(highest, from_above(0), c_u)
    c_moved, _ = here.dual_columns(c_p, c_u, gathered_ref[0])
    sent = (from_below(0) + STEP_DUAL * turn(c_u, -2), from_below(1), from_below(2))
    c_moved = [jnp.where(lowest, s, m) for s, m in zip(sent, c_moved)]
    c_dual = here.project(c_moved, here.columns_inside)

    duals = {x: [dual_ref[d, x] for d in range(3)] for x in range(7)}
    bars = {x: bar_ref[x] for x in range(1, 7)}
    primals = {x: primal_ref[x] for x in range(1, 7)}
    top = OWN - 1
    moved = (below[0] + STEP_DUAL * plane(0, 0), below[1], below[2])
    duals[-1] = here.project(moved, here.inside(-1))
    old = dual(top)
    duals[top] = here.dual_plane(old, plane(0, top), above[0], c_u, top)
    sums[0] += change_of(duals[top], old) * (1.0 / STEP_DUAL)
    for x in (0, top):
        u = plane(0, x)
        divergence = duals[x][0] - duals[x - 1][0] + here.across(duals[x], c_dual[2], x)
        primals[x] = updated(u, plane(4, x), divergence)
        bars[x] = 2.0 * primals[x] - u
        sums[0] += change_of([primals[x]], [u]) * (1.0 / STEP_PRIMAL)
    bars[-1] = below[3] + BAR_F * (duals[-1][0] + here.across(duals[-1], c_dual[2], -1))
    bars[OWN] = above[1] - BAR_F * duals[top][0]

    gathered = gathered_ref[1]
    for x in (-1, top):
        gathered = into_columns(gathered, duals[x][2], x)
    known = jnp.where(
        lowest, from_below(3), jnp.where(highest, from_above(1), early_bar(c_u, c_f))
    )
    own_part = jnp.where(highest, 0.0, c_dual[0] + here.columns_across(c_dual, gathered))
    previous = jnp.where(lowest, 0.0, turn(c_dual[0], 2))
    c_bar = known + BAR_F * (own_part - previous)

    gathered = gathered_ref[2]
    for x in (0, top):
        gathered = into_columns(gathered, bars[x], x)
    _, c_end = here.dual_columns(c_dual, c_bar, gathered)
    ends = {x: [dual_end[d, x] for d in range(3)] for x in range(1, 6)}
    for x in (-1, 0, 6, 7):
        ends[x] = here.dual_plane(duals[x], bars[x], bars[x + 1], c_bar, x)
        if x >= 0:
            sums[1] += change_of(ends[x], duals[x]) * (1.0 / STEP_DUAL)
    for x in range(OWN):
        if 2 <= x <= 5:
            u_out[x] = primal_end[x]
        else:
            divergence = ends[x][0] - ends[x - 1][0] + here.across(ends[x], c_end[2], x)
            now = updated(primals[x], plane(4, x), divergence)
            sums[1] += change_of([now], [primals[x]]) * (1.0 / STEP_PRIMAL)
            u_out[x] = now[:ROWS]
        for d in range(3):
            p_out[d, x] = ends[x][d][:ROWS]
    out_lane = lanes_of(8)
    sums_out[...] = jnp.where(
        out_lane == 0, jnp.sum(sums[0]), jnp.where(out_lane == 1, jnp.sum(sums[1]), 0.0)
    )


def shape(*dims):
    return jax.ShapeDtypeStruct(dims, jnp.float32)


def call(kernel, count, outs, scratch=(), specs=None, work=0):
    return pl.pallas_call(
        kernel,
        out_shape=outs,
        in_specs=specs or [VMEM] * count,
        out_specs=jax.tree.map(lambda _: VMEM, outs),
        scratch_shapes=list(scratch),
        compiler_params=pltpu.CompilerParams(vmem_limit_bytes=4 * 2**20),
        cost_estimate=pl.CostEstimate(flops=work, bytes_accessed=work, transcendentals=0),
    )


def trade(first, second, axes):
    count = lax.axis_size(axes)
    outer = [(i, (i + 1 if i % 2 else i - 1) % count) for i in range(count)]
    second = lax.ppermute(second, axes, outer)
    first = lax.ppermute(first, axes, [(i, i ^ 1) for i in range(count)])
    return first, second


STAGES = ((("core", "y"), 12), (("xl", "z", "xh"), (0 * 8 + 5) * 2 + 1))


def settle(rows):
    values = rows[:1, :2]
    for axes, member in STAGES:
        count = lax.axis_size(axes)
        order = [member] + [i for i in range(count) if i != member]
        spread = jnp.broadcast_to(values, (count, 2))
        spread = lax.all_to_all(spread, axes, 0, 0, tiled=True, axis_index_groups=[order])
        values = jnp.sum(spread, axis=0, keepdims=True)
    return values[0, :2]


def on_device(f, u, p):
    inputs = [pltpu.with_memory_space_constraint(v, pltpu.HBM) for v in (u, f, p)]
    columns, u, f, p = call(
        load,
        3,
        (shape(ROWS, LANES), shape(*u.shape), shape(*f.shape), shape(*p.shape)),
        [pltpu.SemaphoreType.DMA((3,))],
        [pl.BlockSpec(memory_space=pltpu.HBM)] * 3,
    )(*inputs)
    columns = lax.ppermute(columns, GZ, [(0, 1), (1, 0)])

    message = shape(10, 8, LANES)
    first_y, second_y = trade(*call(y_faces, 4, (message, message))(u, f, p, columns), GY)

    message = shape(5, ALL_ROWS, LANES)
    halo, columns, first, second = call(
        x_faces,
        6,
        (shape(5, OWN, 8, LANES), shape(ALL_ROWS, LANES), message, message),
        [pltpu.VMEM((10, 8, LANES), jnp.float32)] * 2,
    )(u, f, p, columns, second_y, first_y)
    first, second = trade(first, second, GX)

    planes = shape(OWN, ALL_ROWS, LANES)
    triple = shape(3, OWN, ALL_ROWS, LANES)
    done = call(
        early,
        6,
        (
            triple, planes, planes, triple, shape(OWN, ROWS, LANES),
            shape(3, ALL_ROWS, LANES), shape(2, 8, LANES),
        ),
        [pltpu.VMEM((5, OWN, 8, LANES), jnp.float32)]
        + [pltpu.VMEM((10, 8, LANES), jnp.float32)] * 2,
        work=10**6,
    )(u, f, p, columns, first_y, second_y)
    denoised, dual, sums = call(
        late,
        14,
        (shape(OWN, ROWS, LANES), shape(3, OWN, ROWS, LANES), shape(8, LANES)),
    )(u, f, p, halo, columns, second, first, *done)
    cells = OWN * lax.axis_size(GX) * ROWS * lax.axis_size(GY) * LANES * lax.axis_size(GZ)
    return denoised, dual, jnp.sqrt(settle(sums) / float(cells))


def solution(mesh):
    mesh = Mesh(mesh.devices.reshape(SIZES), ("xl", "z", "core", "y", "xh"))
    placed = (P(GX, GY, GZ), P(GX, GY, GZ), P(None, GX, GY, GZ))
    return jax.shard_map(
        on_device,
        mesh=mesh,
        in_specs=placed,
        out_specs=(P(GX, GY, GZ), P(None, GX, GY, GZ), P()),
        check_vma=False,
    )
```
